128 devices in a mesh: ctx: 16 (over y, x_hi, core), tp: 8 (over x_lo, z).
Axes of the slice: x: 4 (x_hi: 2, x_lo: 2; x = x_hi * 2 + x_lo), y: 4, z: 4, core: 2. Of those that a mesh axis runs over, the one named last changes fastest.
Arguments:
- normed_layer_input: bfloat16 [8192, 8192], P('ctx'), may hold values from -6 to 6
- queries: bfloat16 [8192, 8192], P('ctx', 'tp'), may hold values from -4.5 to 4.5
- keys: bfloat16 [8192, 1024], P('ctx', 'tp'), may hold values from -4.5 to 4.5
- values: bfloat16 [8192, 1024], P('ctx', 'tp'), may hold values from -6 to 6
- output_gradient: bfloat16 [8192, 8192], P('ctx', 'tp'), may hold values from -6 to 6
- positions: int32 [8192], P('ctx'), may hold values from 0 to 4095, as said below
- query_down_weight: bfloat16 [8, 8192], replicated, may hold values from -0.0625 to 0.0625
- query_up_weight: bfloat16 [8, 8192], P(None, 'tp'), may hold values from -0.0625 to 0.0625
- value_down_weight: bfloat16 [8, 8192], replicated, may hold values from -0.0625 to 0.0625
- value_up_weight: bfloat16 [8, 1024], P(None, 'tp'), may hold values from -0.1875 to 0.1875
Outputs:
- query_gradient_rows: bfloat16 [8192, 8192], P('ctx', 'tp')
- grad_keys: bfloat16 [8192, 1024], P('ctx', 'tp')
- value_gradient_rows: bfloat16 [8192, 1024], P('ctx', 'tp')
- grad_a_q: float32 [8, 8192], replicated
- grad_b_q: float32 [8, 8192], P(None, 'tp')
- grad_a_v: float32 [8, 8192], replicated
- grad_b_v: float32 [8, 1024], P(None, 'tp')
The draws below stay inside these ranges and needn't reach their ends.
Inputs may be any that keep to these rules, and one draw needn't show every extreme that they name: `positions`: position ids count up by one from 0 within each packed sample; the first sample fills the first 4096 tokens and no later sample is longer.
All inputs are finite; a program needn't handle non-finite values.
Results may differ from the reference program's by a relative error of at most 0.02.
Values may be sent and summed in bfloat16 or wider, within the bound.
A program may use at most 128 MiB of HBM per device.

```python
import jax
import jax.numpy as jnp
from jax import lax

MODEL_WIDTH = 8192
QUERY_HEADS = 64
KEY_VALUE_HEADS = 8
HEAD_FEATURES = 128
ADAPTER_RANK = 8
SCALE_NUM = 1
SCALE_DEN = 8
TOKENS = 8192
GROUP = 2048
HALF = 1024


def draw_keys(key, part):
    key = jax.random.fold_in(key, 11)
    shape = (TOKENS, KEY_VALUE_HEADS * HEAD_FEATURES)
    base = jnp.clip(jax.random.normal(key, shape), -4.0, 4.0)
    return base.astype(jnp.bfloat16)


def draw_queries(key, part):
    key = jax.random.fold_in(key, 13)
    shape = (TOKENS, QUERY_HEADS * HEAD_FEATURES)
    base = jnp.clip(jax.random.normal(key, shape), -4.0, 4.0)
    return base.astype(jnp.bfloat16)


def draw_positions(key, part):
    key = jax.random.fold_in(key, 23)
    index = jnp.arange(TOKENS, dtype=jnp.int32)
    middle = TOKENS // 2
    spacing = max(8, TOKENS // 64)
    random_starts = jax.random.randint(key, (TOKENS,), 0, spacing) == 0
    starts = jnp.where(index < middle, index == 0, random_starts | (index == middle))
    anchor = lax.cummax(jnp.where(starts, index, 0), axis=0)
    return (index - anchor).astype(jnp.int32)


def block_scale(stream_key, dims, shards, least, largest):
    gain, own = 1.0, jax.random.fold_in(stream_key, 6)
    for dim, blocks in shards:
        heights = jnp.exp(jax.random.uniform(jax.random.fold_in(own, dim), (blocks,), jnp.float32, least / len(shards), largest / len(shards)))
        gain = gain * jnp.repeat(heights, dims[dim] // blocks).reshape([-1 if axis == dim else 1 for axis in range(len(dims))])
    return gain


def normal_values(own_key, extent, deviation, bound, shards=(), kind=jnp.bfloat16):
    drawn = jax.random.normal(own_key, extent, jnp.float32) * deviation
    if len(shards) > 0:
        drawn = block_scale(own_key, extent, shards, -0.22, 0.18) * drawn
    return jnp.clip(drawn, min=-bound, max=bound).astype(kind)


def setup_inputs(seed: int = 0) -> dict:
    arg_keys = jax.random.split(jax.random.key(seed), 11)
    return {
        "normed_layer_input": normal_values(arg_keys[0], (TOKENS, MODEL_WIDTH), 1.0, 6.0, ((0, 16),)),
        "queries": draw_queries(jax.random.fold_in(arg_keys[10], 71), 0),
        "keys": draw_keys(jax.random.fold_in(arg_keys[10], 71), 0),
        "values": normal_values(arg_keys[3], (TOKENS, KEY_VALUE_HEADS * HEAD_FEATURES), 1.0, 6.0, ((0, 16), (1, 8))),
        "output_gradient": normal_values(arg_keys[4], (TOKENS, QUERY_HEADS * HEAD_FEATURES), 1.0, 6.0, ((0, 16), (1, 8))),
        "positions": draw_positions(jax.random.fold_in(arg_keys[10], 71), 0),
        "query_down_weight": normal_values(arg_keys[6], (ADAPTER_RANK, MODEL_WIDTH), MODEL_WIDTH ** -0.5, 0.0625),
        "query_up_weight": normal_values(arg_keys[7], (ADAPTER_RANK, QUERY_HEADS * HEAD_FEATURES), (QUERY_HEADS * HEAD_FEATURES) ** -0.5, 0.0625, ((1, 8),)),
        "value_down_weight": normal_values(arg_keys[8], (ADAPTER_RANK, MODEL_WIDTH), MODEL_WIDTH ** -0.5, 0.0625),
        "value_up_weight": normal_values(arg_keys[9], (ADAPTER_RANK, KEY_VALUE_HEADS * HEAD_FEATURES), (KEY_VALUE_HEADS * HEAD_FEATURES) ** -0.5, 0.1875, ((1, 8),)),
    }


rope_base = 10000.0


def unrotate(grads, positions):
    width = grads.shape[1] // HEAD_FEATURES
    halfdim = HEAD_FEATURES // 2
    split = grads.reshape(grads.shape[0], width, 2, halfdim)
    index = jnp.arange(halfdim, dtype=jnp.float32)
    inverse = jnp.exp(index * (-2.0 / HEAD_FEATURES) * jnp.log(jnp.float32(rope_base)))
    scaled = (positions * SCALE_NUM).astype(jnp.float32) / SCALE_DEN
    angle = scaled[:, None] * inverse[None, :]
    cosine = jnp.cos(angle)[:, None, :]
    sine = jnp.sin(angle)[:, None, :]
    first = split[:, :, 0, :]
    second = split[:, :, 1, :]
    out_first = first * cosine + second * sine
    out_second = second * cosine - first * sine
    return jnp.stack([out_first, out_second], axis=2).reshape(grads.shape)


def group_backward(query, key_block, value_block, upstream):
    scale = HEAD_FEATURES ** -0.5
    length = query.shape[1]
    causal = jnp.tril(jnp.ones((length, length), dtype=bool))
    query_full = query.astype(jnp.float32)
    key_full = key_block.astype(jnp.float32)
    value_full = value_block.astype(jnp.float32)
    upstream_full = upstream.astype(jnp.float32)
    scores = jnp.einsum("gqd,gkd->gqk", query_full, key_full) * scale
    scores = jnp.where(causal[None], scores, -1e30)
    peak = jnp.max(scores, axis=-1, keepdims=True)
    expo = jnp.exp(scores - peak)
    prob = expo / jnp.sum(expo, axis=-1, keepdims=True)
    prob_low = lax.optimization_barrier(prob.astype(jnp.bfloat16)).astype(jnp.float32)
    output = jnp.einsum("gqk,gkd->gqd", prob_low, value_full)
    delta = jnp.sum(upstream_full * output, axis=-1)
    grad_prob = jnp.einsum("gqd,gkd->gqk", upstream_full, value_full)
    grad_score = prob * (grad_prob - delta[..., None])
    grad_score = lax.optimization_barrier(grad_score.astype(jnp.bfloat16)).astype(jnp.float32)
    grad_query = jnp.einsum("gqk,gkd->gqd", grad_score, key_full) * scale
    grad_key = jnp.einsum("gqk,gqd->gkd", grad_score, query_full) * scale
    grad_value = jnp.einsum("gqk,gqd->gkd", prob_low, upstream_full)
    return grad_query, grad_key, grad_value


def head_block(array, index):
    start = (index * HEAD_FEATURES).astype(jnp.int32)
    return lax.dynamic_slice_in_dim(array, start, HEAD_FEATURES, 1)


def reference(normed_layer_input, queries, keys, values, output_gradient, positions, query_down_weight, query_up_weight, value_down_weight, value_up_weight):
    total = queries.shape[0]
    groups = total // GROUP
    repeat = QUERY_HEADS // KEY_VALUE_HEADS

    def kv_head(index, offset):
        key_rolled = jnp.roll(head_block(keys, index), -offset, axis=0).reshape(groups, GROUP, HEAD_FEATURES)
        value_rolled = jnp.roll(head_block(values, index), -offset, axis=0).reshape(groups, GROUP, HEAD_FEATURES)

        def per_query(carry, member):
            head = index * repeat + member
            query_rolled = jnp.roll(head_block(queries, head), -offset, axis=0).reshape(groups, GROUP, HEAD_FEATURES)
            upstream = jnp.roll(head_block(output_gradient, head), -offset, axis=0).reshape(groups, GROUP, HEAD_FEATURES)
            grad_query, grad_key, grad_value = group_backward(query_rolled, key_rolled, value_rolled, upstream)
            grad_query = jnp.roll(grad_query.reshape(total, HEAD_FEATURES), offset, axis=0)
            return (carry[0] + grad_key, carry[1] + grad_value), grad_query

        zero = jnp.zeros((groups, GROUP, HEAD_FEATURES), jnp.float32)
        sums, query_gradient_rows = lax.scan(per_query, (zero, zero), jnp.arange(repeat, dtype=jnp.int32))
        grad_key = jnp.roll(sums[0].reshape(total, HEAD_FEATURES), offset, axis=0)
        grad_value = jnp.roll(sums[1].reshape(total, HEAD_FEATURES), offset, axis=0)
        return query_gradient_rows, grad_key, grad_value

    plain = lax.map(lambda index: kv_head(index, 0), jnp.arange(KEY_VALUE_HEADS // 2, dtype=jnp.int32))
    moved = lax.map(lambda index: kv_head(index, HALF), jnp.arange(KEY_VALUE_HEADS // 2, KEY_VALUE_HEADS, dtype=jnp.int32))
    query_grad = jnp.concatenate([plain[0], moved[0]], axis=0).reshape(QUERY_HEADS, total, HEAD_FEATURES)
    key_grad = jnp.concatenate([plain[1], moved[1]], axis=0)
    value_grad = jnp.concatenate([plain[2], moved[2]], axis=0)
    query_grad = jnp.transpose(query_grad, (1, 0, 2)).reshape(total, QUERY_HEADS * HEAD_FEATURES)
    key_grad = jnp.transpose(key_grad, (1, 0, 2)).reshape(total, KEY_VALUE_HEADS * HEAD_FEATURES)
    value_grad = jnp.transpose(value_grad, (1, 0, 2)).reshape(total, KEY_VALUE_HEADS * HEAD_FEATURES)
    query_gradient_rows = unrotate(query_grad, positions).astype(jnp.bfloat16)
    grad_keys = unrotate(key_grad, positions).astype(jnp.bfloat16)
    value_gradient_rows = value_grad.astype(jnp.bfloat16)
    query_hidden_gradient = jnp.dot(normed_layer_input, query_down_weight.T, preferred_element_type=jnp.float32).astype(jnp.bfloat16)
    value_hidden_gradient = jnp.dot(normed_layer_input, value_down_weight.T, preferred_element_type=jnp.float32).astype(jnp.bfloat16)
    grad_b_q = jnp.dot(query_hidden_gradient.T, query_gradient_rows, preferred_element_type=jnp.float32)
    grad_b_v = jnp.dot(value_hidden_gradient.T, value_gradient_rows, preferred_element_type=jnp.float32)
    query_pullback = jnp.dot(query_gradient_rows, query_up_weight.T, preferred_element_type=jnp.float32)
    value_pullback = jnp.dot(value_gradient_rows, value_up_weight.T, preferred_element_type=jnp.float32)
    wide_in = normed_layer_input.astype(jnp.float32)
    grad_a_q = jnp.dot(query_pullback.T, wide_in, precision=lax.Precision.HIGHEST)
    grad_a_v = jnp.dot(value_pullback.T, wide_in, precision=lax.Precision.HIGHEST)
    return (query_gradient_rows, grad_keys, value_gradient_rows, grad_a_q, grad_b_q, grad_a_v, grad_b_v)
```

```python
import functools
import math

import jax
import jax.numpy as jnp
from jax import lax
from jax.experimental import pallas as pl
from jax.experimental.pallas import tpu as pltpu
from jax.sharding import PartitionSpec as P

QUERY_HEADS = 64
KEY_VALUE_HEADS = 8
FEATURES = 128
RANK = 8
SCALE_NUM = 1
SCALE_DEN = 8
ROPE_BASE = 10000.0
PLACES = 4
CHUNK = 256
HEADS = QUERY_HEADS // KEY_VALUE_HEADS
SCALE = FEATURES**-0.5
SCALE_LOG2 = SCALE * math.log2(math.e)

F32 = jnp.float32
BF16 = jnp.bfloat16
MESH = pl.DeviceIdType.MESH

DIRECT = {0: (1, 2), 1: (3,), 2: (3,), 3: ()}
HANDED = {2: (0, 3), 3: (1, 2)}


def nt(a, b):
    return lax.dot_general(a, b, (((1,), (1,)), ((), ())), preferred_element_type=F32)


def nn(a, b):
    return jnp.dot(a, b, preferred_element_type=F32)


def fold(a, op):
    return op(a.reshape(a.shape[0] // 8, 8, a.shape[1]), axis=0)


def kernel(
    n_ctx,
    n_tp,
    rows,
    x_hbm,
    q_hbm,
    k_hbm,
    v_hbm,
    do_hbm,
    pos_ref,
    dq_down_ref,
    up_q_ref,
    dv_down_ref,
    up_v_ref,
    dq_hbm,
    gk_ref,
    gv_ref,
    gaq_ref,
    gbq_ref,
    gav_ref,
    gbv_ref,
    xs,
    kall,
    vall,
    ktr,
    qs,
    dos,
    prob,
    work,
    recip,
    dqs,
    dv_out,
    dv_in,
    dk_out,
    dk_in,
    dv_own,
    dk_own,
    ctab,
    stab,
    down,
    hid,
    pulls,
    rs_out,
    rs_in,
    ag,
    full,
    load_sem,
    xsem,
    out_sem,
    own_sem,
    k_send,
    k_recv,
    v_send,
    v_recv,
    dv_send,
    dv_recv,
    dk_send,
    dk_recv,
    pull_send,
    pull_recv,
    rs_send,
    rs_recv,
    ag_send,
    ag_recv,
    full_send,
    full_recv,
):
    c = lax.axis_index("ctx")
    t = lax.axis_index("tp")
    halves = rows // CHUNK
    width = HEADS * FEATURES
    shifted = jnp.where(t >= n_tp // 2, PLACES // 2, 0)
    place = lax.rem(c + shifted, PLACES)

    def member(j):
        return lax.rem(c - place + j + n_ctx, n_ctx)

    barrier = pltpu.get_barrier_semaphore()
    for d in range(1, n_ctx):
        pl.semaphore_signal(barrier, inc=1, device_id={"ctx": lax.rem(c + d, n_ctx)}, device_id_type=MESH)
    for d in range(1, n_tp):
        pl.semaphore_signal(barrier, inc=1, device_id={"tp": lax.rem(t + d, n_tp)}, device_id_type=MESH)

    own = pl.ds(pl.multiple_of(place * rows, rows), rows)
    own_k = pltpu.make_async_copy(k_hbm, kall.at[own], own_sem.at[0])
    own_v = pltpu.make_async_copy(v_hbm, vall.at[own], own_sem.at[1])
    own_k.start()
    loads = []
    for j in range(halves):
        for h in range(HEADS):
            for n, (src, dst) in enumerate(((q_hbm, qs), (do_hbm, dos))):
                loads.append(
                    pltpu.make_async_copy(
                        src.at[pl.ds(j * CHUNK, CHUNK), pl.ds(h * FEATURES, FEATURES)],
                        dst.at[j, pl.ds(h * CHUNK, CHUNK)],
                        load_sem.at[n, j * HEADS + h],
                    )
                )
    part = rows // xs_parts
    xloads = [
        pltpu.make_async_copy(x_hbm.at[pl.ds(i * part, part)], xs.at[pl.ds(i * part, part)], xsem.at[i])
        for i in range(xs_parts)
    ]
    xloads[0].start()
    own_v.start()
    for copy in loads:
        copy.start()
    for copy in xloads[1:]:
        copy.start()

    pl.semaphore_wait(barrier, n_ctx + n_tp - 2)

    def block(b):
        return pl.ds(b * rows, rows)

    def send_block(src, dst, b, to, send, recv):
        return pltpu.make_async_remote_copy(
            src_ref=src,
            dst_ref=dst.at[block(b)],
            send_sem=send,
            recv_sem=recv.at[b],
            device_id={"ctx": member(to)},
            device_id_type=MESH,
        )

    for p in range(PLACES):

        @pl.when(place == p)
        def _(p=p):
            for src, dst, send, recv in ((k_hbm, kall, k_send, k_recv), (v_hbm, vall, v_send, v_recv)):
                for i, to in enumerate(DIRECT[p]):
                    send_block(src, dst, p, to, send.at[i], recv).start()

    lane = lax.broadcasted_iota(jnp.int32, (FEATURES, rows), 0)
    index = jnp.where(lane < FEATURES // 2, lane, lane - FEATURES // 2).astype(F32)
    inverse = jnp.exp(index * (-2.0 / FEATURES) * jnp.log(F32(ROPE_BASE)))
    angle = ((pos_ref[...] * SCALE_NUM).astype(F32) / SCALE_DEN) * inverse
    ctab[...] = jnp.cos(angle).T
    stab[...] = jnp.where(lane < FEATURES // 2, jnp.sin(angle), -jnp.sin(angle)).T

    down[...] = jnp.concatenate([dq_down_ref[...].astype(F32), dv_down_ref[...].astype(F32)], axis=0).astype(BF16)
    for i in range(xs_parts):
        xloads[i].wait()
        h = nt(xs[pl.ds(i * part, part), :], down[...])
        h = jnp.concatenate([h, jnp.zeros((part, FEATURES - 2 * RANK), F32)], axis=1)
        hid[:, pl.ds(i * part, part)] = h.T[: 2 * RANK].astype(BF16)
    for copy in loads:
        copy.wait()
    own_k.wait()
    own_v.wait()

    causal = lax.broadcasted_iota(jnp.int32, (CHUNK, CHUNK), 0) <= lax.broadcasted_iota(jnp.int32, (CHUNK, CHUNK), 1)

    def unrotate(a, tokens):
        return a * ctab[tokens, :] + pltpu.roll(a, FEATURES // 2, 1) * stab[tokens, :]

    def attention(p):
        def tiles(j):
            return halves * p + j + 1

        def take(i):
            return pl.ds(i * CHUNK, CHUNK)

        def arrive(dst, send, recv, kind):
            src = k_hbm if kind == 0 else v_hbm
            if p in HANDED:
                b, to = HANDED[p]
                send_block(src, dst, b, to, send.at[2], recv).wait_recv()
                send_block(dst.at[block(b)], dst, b, to, send.at[2], recv).start()
            for b in range(p):
                if p not in HANDED or b != HANDED[p][0]:
                    send_block(src, dst, b, b, send.at[0], recv).wait_recv()

        arrive(kall, k_send, k_recv, 0)
        for i in range(halves * (p + 1)):
            ktr[:, take(i)] = kall[take(i), :].astype(F32).T.astype(BF16)

        @pl.loop(0, HEADS)
        def _(h):
            cols = pl.ds(pl.multiple_of(h * CHUNK, CHUNK), CHUNK)
            for j in range(halves):
                query = qs[j, cols, :]
                peak = None
                for i in range(tiles(j)):
                    s = nt(kall[take(i), :], query)
                    if i == tiles(j) - 1:
                        s = jnp.where(causal, s, -1e30)
                    work[j, take(i), :] = s
                    top = fold(s, jnp.max)
                    peak = top if peak is None else jnp.maximum(peak, top)
                peak = jnp.max(peak, axis=0, keepdims=True) * SCALE_LOG2
                total = jnp.zeros((8, CHUNK), F32)
                for i in range(tiles(j)):
                    e = jnp.exp2(work[j, take(i), :] * SCALE_LOG2 - peak)
                    total = total + fold(e, jnp.sum)
                    prob[j, take(i), cols] = e.astype(BF16)
                inv = 1.0 / jnp.sum(total, axis=0, keepdims=True)
                recip[j * HEADS + h] = inv
                column = jnp.broadcast_to(inv, (FEATURES, CHUNK)).T
                dos[j, cols, :] = (dos[j, cols, :].astype(F32) * column).astype(BF16)

        arrive(vall, v_send, v_recv, 1)

        def key_terms(right, scale, outs, send, recv, kept):
            def finish(a):
                return a if scale is None else a * scale

            for b in range(p):
                a = nn(prob[0, block(b), :], right[0])
                for j in range(1, halves):
                    a = a + nn(prob[j, block(b), :], right[j])
                outs[b] = finish(a).astype(BF16)
                term_copy(outs, send, recv, p, b).start()
            for i in range(halves):
                a = None
                for j in range(i, halves):
                    m = nn(prob[j, take(halves * p + i), :], right[j])
                    a = m if a is None else a + m
                kept[take(i), :] = finish(a)

        key_terms(dos, None, dv_out, dv_send, dv_in_recv, dv_own)

        @pl.loop(0, HEADS)
        def _(h):
            cols = pl.ds(pl.multiple_of(h * CHUNK, CHUNK), CHUNK)
            for j in range(halves):
                up = dos[j, cols, :]
                total = jnp.zeros((8, CHUNK), F32)
                for i in range(tiles(j)):
                    g = nt(vall[take(i), :], up)
                    total = total + fold(prob[j, take(i), cols].astype(F32) * g, jnp.sum)
                    work[j, take(i), :] = g
                delta = jnp.sum(total, axis=0, keepdims=True) * recip[j * HEADS + h]
                grad = jnp.zeros((FEATURES, CHUNK), F32)
                for i in range(tiles(j)):
                    ds = (prob[j, take(i), cols].astype(F32) * (work[j, take(i), :] - delta)).astype(BF16)
                    prob[j, take(i), cols] = ds
                    grad = grad + nn(ktr[:, take(i)], ds)
                out = unrotate(grad.T * SCALE, take(j))
                dqs[take(j), pl.ds(pl.multiple_of(h * FEATURES, FEATURES), FEATURES)] = out.astype(BF16)

        pltpu.make_async_copy(dqs, dq_hbm, out_sem.at[0]).start()

        total = dv_own[...]
        for src in range(p + 1, PLACES):
            term_copy(dv_out, dv_send, dv_in_recv, src, p).wait_recv()
            total = total + dv_in[src - 1].astype(F32)
        gv_ref[...] = total.astype(BF16)

        pulls[t] = jnp.concatenate([nt(up_q_ref[...], dqs[...]), nt(up_v_ref[...], gv_ref[...])], axis=0)
        for d in range(1, n_tp):
            pull_copy(d).start()

        key_terms(qs, SCALE, dk_out, dk_send, dk_in_recv, dk_own)

    dv_in_recv = (dv_in, dv_recv)
    dk_in_recv = (dk_in, dk_recv)

    def term_copy(outs, send, into, src, b):
        dst, recv = into
        return pltpu.make_async_remote_copy(
            src_ref=outs.at[b],
            dst_ref=dst.at[src - 1],
            send_sem=send.at[b],
            recv_sem=recv.at[src - 1],
            device_id={"ctx": member(b)},
            device_id_type=MESH,
        )

    def pull_copy(d):
        return pltpu.make_async_remote_copy(
            src_ref=pulls.at[t],
            dst_ref=pulls.at[t],
            send_sem=pull_send.at[d],
            recv_sem=pull_recv.at[t],
            device_id={"tp": lax.rem(t + d, n_tp)},
            device_id_type=MESH,
        )

    def pull_arrival(s):
        return pltpu.make_async_remote_copy(
            src_ref=pulls.at[s],
            dst_ref=pulls.at[s],
            send_sem=pull_send.at[0],
            recv_sem=pull_recv.at[s],
            device_id={"tp": s},
            device_id_type=MESH,
        )

    for p in range(PLACES):
        pl.when(place == p)(functools.partial(attention, p))

    hidden = hid[...]
    gb = nn(hidden, dqs[...])[:RANK]
    gbv = nn(hidden, gv_ref[...])[RANK:]
    for i in range(n_ctx):
        if i < HEADS:
            rs_out[i, RANK:, :] = gb[:, i * FEATURES : (i + 1) * FEATURES]
        elif i == HEADS:
            rs_out[i, RANK:, :] = gbv
        else:
            rs_out[i, RANK:, :] = jnp.zeros((RANK, FEATURES), F32)

    for d in range(1, n_tp):
        pull_arrival(lax.rem(t + d, n_tp)).wait_recv()
    pull = pulls[0]
    for s in range(1, n_tp):
        pull = pull + pulls[s]
    high = pull.astype(BF16)
    low = (pull - high.astype(F32)).astype(BF16)
    share = xs[:, pl.ds(pl.multiple_of(t * width, width), width)]
    ga = nn(high, share) + nn(low, share)
    for i in range(n_ctx):
        a, b = divmod(i, HEADS)
        rs_out[i, :RANK, :] = ga[a * RANK : (a + 1) * RANK, b * FEATURES : (b + 1) * FEATURES]

    def rs_copy(d):
        peer = lax.rem(c + d, n_ctx)
        return pltpu.make_async_remote_copy(
            src_ref=rs_out.at[peer],
            dst_ref=rs_in.at[c],
            send_sem=rs_send.at[d],
            recv_sem=rs_recv.at[c],
            device_id={"ctx": peer},
            device_id_type=MESH,
        )

    def rs_arrival(s):
        return pltpu.make_async_remote_copy(
            src_ref=rs_out.at[s],
            dst_ref=rs_in.at[s],
            send_sem=rs_send.at[0],
            recv_sem=rs_recv.at[s],
            device_id={"ctx": s},
            device_id_type=MESH,
        )

    for d in range(1, n_ctx):
        rs_copy(d).start()

    for p in range(PLACES):

        @pl.when(place == p)
        def _(p=p):
            total = dk_own[...]
            for src in range(p + 1, PLACES):
                term_copy(dk_out, dk_send, dk_in_recv, src, p).wait_recv()
                total = total + dk_in[src - 1].astype(F32)
            gk_ref[...] = unrotate(total, pl.ds(0, rows)).astype(BF16)

    rs_in[c] = rs_out[c]
    for d in range(1, n_ctx):
        rs_arrival(lax.rem(c + d, n_ctx)).wait_recv()
    tile = rs_in[0]
    for s in range(1, n_ctx):
        tile = tile + rs_in[s]
    ag[c] = tile

    def ag_copy(d):
        return pltpu.make_async_remote_copy(
            src_ref=ag.at[c],
            dst_ref=ag.at[c],
            send_sem=ag_send.at[d],
            recv_sem=ag_recv.at[c],
            device_id={"ctx": lax.rem(c + d, n_ctx)},
            device_id_type=MESH,
        )

    def ag_arrival(s):
        return pltpu.make_async_remote_copy(
            src_ref=ag.at[s],
            dst_ref=ag.at[s],
            send_sem=ag_send.at[0],
            recv_sem=ag_recv.at[s],
            device_id={"ctx": s},
            device_id_type=MESH,
        )

    for d in range(1, n_ctx):
        ag_copy(d).start()
    for d in range(1, n_ctx):
        ag_arrival(lax.rem(c + d, n_ctx)).wait_recv()
    slices = []
    for b in range(HEADS):
        slices.append(jnp.concatenate([ag[b, :RANK, :], ag[HEADS + b, :RANK, :]], axis=0))
    full[t] = jnp.concatenate(slices, axis=1).astype(BF16)

    def full_copy(d):
        return pltpu.make_async_remote_copy(
            src_ref=full.at[t],
            dst_ref=full.at[t],
            send_sem=full_send.at[d],
            recv_sem=full_recv.at[t],
            device_id={"tp": lax.rem(t + d, n_tp)},
            device_id_type=MESH,
        )

    def full_arrival(s):
        return pltpu.make_async_remote_copy(
            src_ref=full.at[s],
            dst_ref=full.at[s],
            send_sem=full_send.at[0],
            recv_sem=full_recv.at[s],
            device_id={"tp": s},
            device_id_type=MESH,
        )

    for d in range(1, n_tp):
        full_copy(d).start()
    for b in range(HEADS):
        gbq_ref[:, b * FEATURES : (b + 1) * FEATURES] = ag[b, RANK:, :]
    gbv_ref[...] = ag[HEADS, RANK:, :]
    for d in range(1, n_tp):
        full_arrival(lax.rem(t + d, n_tp)).wait_recv()
    for s in range(n_tp):
        whole = full[s].astype(F32)
        gaq_ref[:, s * width : (s + 1) * width] = whole[:RANK]
        gav_ref[:, s * width : (s + 1) * width] = whole[RANK:]

    for d in range(1, n_ctx):
        rs_copy(d).wait_send()
        ag_copy(d).wait_send()
    for d in range(1, n_tp):
        pull_copy(d).wait_send()
        full_copy(d).wait_send()
    for p in range(PLACES):

        @pl.when(place == p)
        def _(p=p):
            for src, dst, send, recv in ((k_hbm, kall, k_send, k_recv), (v_hbm, vall, v_send, v_recv)):
                for i, to in enumerate(DIRECT[p]):
                    send_block(src, dst, p, to, send.at[i], recv).wait_send()
                if p in HANDED:
                    b, to = HANDED[p]
                    send_block(dst.at[block(b)], dst, b, to, send.at[2], recv).wait_send()
            for b in range(p):
                term_copy(dv_out, dv_send, dv_in_recv, p, b).wait_send()
                term_copy(dk_out, dk_send, dk_in_recv, p, b).wait_send()

    pltpu.make_async_copy(dqs, dq_hbm, out_sem.at[0]).wait()


xs_parts = 4


def shards(x, q, k, v, do, positions, down_q, up_q, down_v, up_v):
    n_ctx, n_tp = lax.axis_size("ctx"), lax.axis_size("tp")
    rows = q.shape[0]
    model = x.shape[1]
    keys = PLACES * rows
    halves = rows // CHUNK
    width = HEADS * FEATURES
    any_spec = pl.BlockSpec(memory_space=pl.ANY)
    vmem = pl.BlockSpec(memory_space=pltpu.VMEM)
    dma = pltpu.SemaphoreType.DMA
    terms = pltpu.VMEM((PLACES - 1, rows, FEATURES), BF16)
    whole = pltpu.VMEM((rows, FEATURES), F32)
    return pl.pallas_call(
        functools.partial(kernel, n_ctx, n_tp, rows),
        out_shape=(
            jax.ShapeDtypeStruct((rows, width), BF16),
            jax.ShapeDtypeStruct((rows, FEATURES), BF16),
            jax.ShapeDtypeStruct((rows, FEATURES), BF16),
            jax.ShapeDtypeStruct((RANK, model), F32),
            jax.ShapeDtypeStruct((RANK, width), F32),
            jax.ShapeDtypeStruct((RANK, model), F32),
            jax.ShapeDtypeStruct((RANK, FEATURES), F32),
        ),
        in_specs=[any_spec] * 5 + [vmem] * 5,
        out_specs=(any_spec,) + (vmem,) * 6,
        scratch_shapes=[
            pltpu.VMEM((rows, model), BF16),
            pltpu.VMEM((keys, FEATURES), BF16),
            pltpu.VMEM((keys, FEATURES), BF16),
            pltpu.VMEM((FEATURES, keys), BF16),
            pltpu.VMEM((halves, HEADS * CHUNK, FEATURES), BF16),
            pltpu.VMEM((halves, HEADS * CHUNK, FEATURES), BF16),
            pltpu.VMEM((halves, keys, HEADS * CHUNK), BF16),
            pltpu.VMEM((halves, keys, CHUNK), F32),
            pltpu.VMEM((halves * HEADS, 1, CHUNK), F32),
            pltpu.VMEM((rows, width), BF16),
            terms,
            terms,
            terms,
            terms,
            whole,
            whole,
            whole,
            whole,
            pltpu.VMEM((2 * RANK, model), BF16),
            pltpu.VMEM((2 * RANK, rows), BF16),
            pltpu.VMEM((n_tp, 2 * RANK, rows), F32),
            pltpu.VMEM((n_ctx, 2 * RANK, FEATURES), F32),
            pltpu.VMEM((n_ctx, 2 * RANK, FEATURES), F32),
            pltpu.VMEM((n_ctx, 2 * RANK, FEATURES), F32),
            pltpu.VMEM((n_tp, 2 * RANK, width), BF16),
            dma((2, halves * HEADS)),
            dma((xs_parts,)),
            dma((1,)),
            dma((2,)),
            dma((3,)),
            dma((PLACES,)),
            dma((3,)),
            dma((PLACES,)),
            dma((PLACES - 1,)),
            dma((PLACES - 1,)),
            dma((PLACES - 1,)),
            dma((PLACES - 1,)),
            dma((n_tp,)),
            dma((n_tp,)),
            dma((n_ctx,)),
            dma((n_ctx,)),
            dma((n_ctx,)),
            dma((n_ctx,)),
            dma((n_tp,)),
            dma((n_tp,)),
        ],
        compiler_params=pltpu.CompilerParams(
            collective_id=0, has_side_effects=True, vmem_limit_bytes=56 * 1024 * 1024
        ),
        cost_estimate=pl.CostEstimate(flops=12 * 10**9, bytes_accessed=16 * 10**6, transcendentals=8 * 10**6),
    )(x, q, k, v, do, positions.reshape(1, rows), down_q, up_q, down_v, up_v)


def solution(mesh):
    in_specs = (
        P("ctx", None),
        P("ctx", "tp"),
        P("ctx", "tp"),
        P("ctx", "tp"),
        P("ctx", "tp"),
        P("ctx"),
        P(),
        P(None, "tp"),
        P(),
        P(None, "tp"),
    )
    out_specs = (
        P("ctx", "tp"),
        P("ctx", "tp"),
        P("ctx", "tp"),
        P(),
        P(None, "tp"),
        P(),
        P(None, "tp"),
    )
    return jax.shard_map(shards, mesh=mesh, in_specs=in_specs, out_specs=out_specs, check_vma=False)
```

```python
import functools
import math

import jax
import jax.numpy as jnp
from jax import lax
from jax.experimental import pallas as pl
from jax.experimental.pallas import tpu as pltpu
from jax.sharding import PartitionSpec as P

QUERY_HEADS = 64
KEY_VALUE_HEADS = 8
FEATURES = 128
RANK = 8
SCALE_NUM = 1
SCALE_DEN = 8
ROPE_BASE = 10000.0
PLACES = 4
CHUNK = 256
HEADS = QUERY_HEADS // KEY_VALUE_HEADS
SCALE = FEATURES**-0.5
SCALE_LOG2 = SCALE * math.log2(math.e)

F32 = jnp.float32
BF16 = jnp.bfloat16
MESH = pl.DeviceIdType.MESH

DIRECT = {0: (1, 2), 1: (3,), 2: (3,), 3: ()}
HANDED = {2: (0, 3), 3: (1, 2)}


def nt(a, b):
    return lax.dot_general(a, b, (((1,), (1,)), ((), ())), preferred_element_type=F32)


def nn(a, b):
    return jnp.dot(a, b, preferred_element_type=F32)


def fold(a, op):
    return op(a.reshape(a.shape[0] // 8, 8, a.shape[1]), axis=0)


def kernel(
    n_ctx,
    n_tp,
    rows,
    x_hbm,
    q_hbm,
    k_hbm,
    v_hbm,
    do_hbm,
    pos_ref,
    dq_down_ref,
    up_q_ref,
    dv_down_ref,
    up_v_ref,
    dq_hbm,
    gk_hbm,
    gv_hbm,
    gb_hbm,
    full,
    xs,
    xr,
    kall,
    vall,
    ktr,
    vtr,
    qs,
    dos,
    prob,
    work,
    deltas,
    dqs,
    dv_out,
    dv_in,
    dk_out,
    dk_in,
    dv_own,
    dk_own,
    ctab,
    stab,
    down,
    hid,
    pulls,
    rs_out,
    rs_in,
    ag,
    mine,
    gk_ref,
    gv_ref,
    gb_ref,
    load_sem,
    xsem,
    out_sem,
    own_sem,
    k_send,
    k_recv,
    v_send,
    v_recv,
    dv_send,
    dv_recv,
    dk_send,
    dk_recv,
    pull_send,
    pull_recv,
    rs_send,
    rs_recv,
    ag_send,
    ag_recv,
    full_send,
    full_recv,
    hid_send,
    hid_recv,
):
    c = lax.axis_index("ctx")
    t = lax.axis_index("tp")
    halves = rows // CHUNK
    width = HEADS * FEATURES
    shifted = jnp.where(t >= n_tp // 2, PLACES // 2, 0)
    place = lax.rem(c + shifted, PLACES)

    def member(j):
        return lax.rem(c - place + j + n_ctx, n_ctx)

    barrier = pltpu.get_barrier_semaphore()
    for d in range(1, n_ctx):
        pl.semaphore_signal(barrier, inc=1, device_id={"ctx": lax.rem(c + d, n_ctx)}, device_id_type=MESH)
    for d in range(1, n_tp):
        pl.semaphore_signal(barrier, inc=1, device_id={"tp": lax.rem(t + d, n_tp)}, device_id_type=MESH)

    own = pl.ds(pl.multiple_of(place * rows, rows), rows)
    own_k = pltpu.make_async_copy(k_hbm, kall.at[own], own_sem.at[0])
    own_v = pltpu.make_async_copy(v_hbm, vall.at[own], own_sem.at[1])
    own_k.start()
    loads = []
    for j in range(halves):
        for h in range(HEADS):
            for n, (src, dst) in enumerate(((q_hbm, qs), (do_hbm, dos))):
                loads.append(
                    pltpu.make_async_copy(
                        src.at[pl.ds(j * CHUNK, CHUNK), pl.ds(h * FEATURES, FEATURES)],
                        dst.at[j, pl.ds(h * CHUNK, CHUNK)],
                        load_sem.at[n, j * HEADS + h],
                    )
                )
    part = rows // n_tp
    load_rows = pltpu.make_async_copy(x_hbm.at[pl.ds(pl.multiple_of(t * part, part), part)], xr, xsem.at[0])
    load_share = pltpu.make_async_copy(x_hbm.at[:, pl.ds(pl.multiple_of(t * width, width), width)], xs, xsem.at[1])
    load_rows.start()
    for copy in loads:
        copy.start()
    own_v.start()
    load_share.start()

    pl.semaphore_wait(barrier, n_ctx + n_tp - 2)

    def block(b):
        return pl.ds(b * rows, rows)

    def send_block(src, dst, b, to, send, recv):
        return pltpu.make_async_remote_copy(
            src_ref=src,
            dst_ref=dst.at[block(b)],
            send_sem=send,
            recv_sem=recv.at[b],
            device_id={"ctx": member(to)},
            device_id_type=MESH,
        )

    for p in range(PLACES):

        @pl.when(place == p)
        def _(p=p):
            for i, to in enumerate(DIRECT[p]):
                send_block(k_hbm, kall, p, to, k_send.at[i], k_recv).start()

    lane = lax.broadcasted_iota(jnp.int32, (FEATURES, rows), 0)
    index = jnp.where(lane < FEATURES // 2, lane, lane - FEATURES // 2).astype(F32)
    inverse = jnp.exp(index * (-2.0 / FEATURES) * jnp.log(F32(ROPE_BASE)))
    angle = ((pos_ref[...] * SCALE_NUM).astype(F32) / SCALE_DEN) * inverse
    ctab[...] = jnp.cos(angle).T
    stab[...] = jnp.where(lane < FEATURES // 2, jnp.sin(angle), -jnp.sin(angle)).T

    ones = lax.broadcasted_iota(jnp.int32, (2 * RANK, PLACES * rows), 0) == 0
    vtr[FEATURES:, :] = jnp.where(ones, 1.0, 0.0).astype(BF16)
    down[...] = jnp.concatenate([dq_down_ref[...].astype(F32), dv_down_ref[...].astype(F32)], axis=0).astype(BF16)
    load_rows.wait()
    h = nt(xr[...], down[...])
    hid[t] = jnp.concatenate([h, jnp.zeros((part, FEATURES - 2 * RANK), F32)], axis=1).astype(BF16)

    def hid_copy(d):
        return pltpu.make_async_remote_copy(
            src_ref=hid.at[t],
            dst_ref=hid.at[t],
            send_sem=hid_send.at[d],
            recv_sem=hid_recv.at[t],
            device_id={"tp": lax.rem(t + d, n_tp)},
            device_id_type=MESH,
        )

    def hid_arrival(s):
        return pltpu.make_async_remote_copy(
            src_ref=hid.at[s],
            dst_ref=hid.at[s],
            send_sem=hid_send.at[0],
            recv_sem=hid_recv.at[s],
            device_id={"tp": s},
            device_id_type=MESH,
        )

    for d in range(1, n_tp):
        hid_copy(d).start()
    for p in range(PLACES):

        @pl.when(place == p)
        def _(p=p):
            for i, to in enumerate(DIRECT[p]):
                send_block(v_hbm, vall, p, to, v_send.at[i], v_recv).start()

    for copy in loads:
        copy.wait()
    own_k.wait()
    own_v.wait()

    causal = lax.broadcasted_iota(jnp.int32, (CHUNK, CHUNK), 0) <= lax.broadcasted_iota(jnp.int32, (CHUNK, CHUNK), 1)

    def unrotate(a, tokens):
        return a * ctab[tokens, :] + pltpu.roll(a, FEATURES // 2, 1) * stab[tokens, :]

    def attention(p):
        def tiles(j):
            return halves * p + j + 1

        def take(i):
            return pl.ds(i * CHUNK, CHUNK)

        def arrive(dst, send, recv, kind):
            src = k_hbm if kind == 0 else v_hbm
            if p in HANDED:
                b, to = HANDED[p]
                send_block(src, dst, b, to, send.at[2], recv).wait_recv()
                send_block(dst.at[block(b)], dst, b, to, send.at[2], recv).start()
            for b in range(p):
                if p not in HANDED or b != HANDED[p][0]:
                    send_block(src, dst, b, b, send.at[0], recv).wait_recv()

        arrive(kall, k_send, k_recv, 0)
        for i in range(halves * (p + 1)):
            ktr[:, take(i)] = kall[take(i), :].astype(F32).T.astype(BF16)

        @pl.loop(0, HEADS)
        def _(h):
            cols = pl.ds(pl.multiple_of(h * CHUNK, CHUNK), CHUNK)
            for j in range(halves):
                query = qs[j, cols, :]
                last = tiles(j) * CHUNK - CHUNK
                starts = list(range(0, last, 2 * CHUNK)) + [last]
                peak = None
                for a, b in zip(starts, starts[1:] + [last + CHUNK]):
                    s = nt(kall[a:b, :], query)
                    if a == last:
                        s = jnp.where(causal, s, -1e30)
                    work[j, a:b, :] = s
                    top = fold(s, jnp.max)
                    peak = top if peak is None else jnp.maximum(peak, top)
                peak = jnp.max(peak, axis=0, keepdims=True) * SCALE_LOG2
                for i in range(tiles(j)):
                    prob[j, take(i), cols] = jnp.exp2(work[j, take(i), :] * SCALE_LOG2 - peak).astype(BF16)

        arrive(vall, v_send, v_recv, 1)
        for i in range(halves * (p + 1)):
            vtr[:FEATURES, take(i)] = vall[take(i), :].astype(F32).T.astype(BF16)

        @pl.loop(0, HEADS)
        def _(h):
            cols = pl.ds(pl.multiple_of(h * CHUNK, CHUNK), CHUNK)
            for j in range(halves):
                length = tiles(j) * CHUNK
                out = nn(vtr[:, :length], prob[j, :length, cols])
                inv = 1.0 / out[FEATURES : FEATURES + 1]
                up = dos[j, cols, :].astype(F32).T * inv
                deltas[j * HEADS + h] = jnp.sum(up * out[:FEATURES], axis=0, keepdims=True) * inv
                dos[j, cols, :] = up.T.astype(BF16)

        key_terms(p, range(p), True, dos, None, dv_out, dv_send, dv_in_recv, dv_own)

        @pl.loop(0, HEADS)
        def _(h):
            cols = pl.ds(pl.multiple_of(h * CHUNK, CHUNK), CHUNK)
            for j in range(halves):
                up = dos[j, cols, :]
                delta = deltas[j * HEADS + h]
                length = tiles(j) * CHUNK
                for a in range(0, length, 4 * CHUNK):
                    b = min(a + 4 * CHUNK, length)
                    g = nt(vall[a:b, :], up)
                    prob[j, a:b, cols] = (prob[j, a:b, cols].astype(F32) * (g - delta)).astype(BF16)
                grad = nn(ktr[:, :length], prob[j, :length, cols])
                out = unrotate(grad.T * SCALE, take(j))
                dqs[take(j), pl.ds(pl.multiple_of(h * FEATURES, FEATURES), FEATURES)] = out.astype(BF16)

        pltpu.make_async_copy(dqs, dq_hbm, out_sem.at[0]).start()

        total = dv_own[...]
        for src in range(p + 1, PLACES):
            term_copy(dv_out, dv_send, dv_in_recv, src, p).wait_recv()
            total = total + dv_in[src - 1].astype(F32)
        gv_ref[...] = total.astype(BF16)
        pltpu.make_async_copy(gv_ref, gv_hbm, out_sem.at[1]).start()

        pulls[t] = jnp.concatenate([nt(up_q_ref[...], dqs[...]), nt(up_v_ref[...], gv_ref[...])], axis=0)
        for d in range(1, n_tp):
            pull_copy(d).start()

        key_terms(p, range(p - 1), False, qs, SCALE, dk_out, dk_send, dk_in_recv, dk_own)

    def key_terms(p, blocks, home, right, scale, outs, send, into, kept):
        def finish(a):
            return a if scale is None else a * scale

        for b in blocks:
            a = nn(prob[0, block(b), :], right[0])
            for j in range(1, halves):
                a = a + nn(prob[j, block(b), :], right[j])
            outs[b] = finish(a).astype(BF16)
            term_copy(outs, send, into, p, b).start()
        if home:
            for i in range(halves):
                a = None
                for j in range(i, halves):
                    m = nn(prob[j, pl.ds((halves * p + i) * CHUNK, CHUNK), :], right[j])
                    a = m if a is None else a + m
                kept[pl.ds(i * CHUNK, CHUNK), :] = finish(a)

    dv_in_recv = (dv_in, dv_recv)
    dk_in_recv = (dk_in, dk_recv)

    def term_copy(outs, send, into, src, b):
        dst, recv = into
        return pltpu.make_async_remote_copy(
            src_ref=outs.at[b],
            dst_ref=dst.at[src - 1],
            send_sem=send.at[b],
            recv_sem=recv.at[src - 1],
            device_id={"ctx": member(b)},
            device_id_type=MESH,
        )

    def pull_copy(d):
        return pltpu.make_async_remote_copy(
            src_ref=pulls.at[t],
            dst_ref=pulls.at[t],
            send_sem=pull_send.at[d],
            recv_sem=pull_recv.at[t],
            device_id={"tp": lax.rem(t + d, n_tp)},
            device_id_type=MESH,
        )

    def pull_arrival(s):
        return pltpu.make_async_remote_copy(
            src_ref=pulls.at[s],
            dst_ref=pulls.at[s],
            send_sem=pull_send.at[0],
            recv_sem=pull_recv.at[s],
            device_id={"tp": s},
            device_id_type=MESH,
        )

    for p in range(PLACES):
        pl.when(place == p)(functools.partial(attention, p))

    for d in range(1, n_tp):
        hid_arrival(lax.rem(t + d, n_tp)).wait_recv()
    hidden = hid[...].astype(F32).reshape(rows, FEATURES).T[: 2 * RANK].astype(BF16)
    gb = nn(hidden, dqs[...])[:RANK]
    gbv = nn(hidden, gv_ref[...])[RANK:]
    for i in range(n_ctx):
        if i < HEADS:
            rs_out[i, RANK:, :] = gb[:, i * FEATURES : (i + 1) * FEATURES]
        elif i == HEADS:
            rs_out[i, RANK:, :] = gbv
        else:
            rs_out[i, RANK:, :] = jnp.zeros((RANK, FEATURES), F32)

    for d in range(1, n_tp):
        pull_arrival(lax.rem(t + d, n_tp)).wait_recv()
    pull = pulls[0]
    for s in range(1, n_tp):
        pull = pull + pulls[s]
    high = pull.astype(BF16)
    low = (pull - high.astype(F32)).astype(BF16)
    load_share.wait()
    ga = nn(high, xs[...]) + nn(low, xs[...])
    for i in range(n_ctx):
        a, b = divmod(i, HEADS)
        rs_out[i, :RANK, :] = ga[a * RANK : (a + 1) * RANK, b * FEATURES : (b + 1) * FEATURES]

    def rs_copy(d):
        peer = lax.rem(c + d, n_ctx)
        return pltpu.make_async_remote_copy(
            src_ref=rs_out.at[peer],
            dst_ref=rs_in.at[c],
            send_sem=rs_send.at[d],
            recv_sem=rs_recv.at[c],
            device_id={"ctx": peer},
            device_id_type=MESH,
        )

    def rs_arrival(s):
        return pltpu.make_async_remote_copy(
            src_ref=rs_out.at[s],
            dst_ref=rs_in.at[s],
            send_sem=rs_send.at[0],
            recv_sem=rs_recv.at[s],
            device_id={"ctx": s},
            device_id_type=MESH,
        )

    for d in range(1, n_ctx):
        rs_copy(d).start()

    for p in range(PLACES):

        @pl.when(place == p)
        def _(p=p):
            key_terms(p, range(max(p - 1, 0), p), True, qs, SCALE, dk_out, dk_send, dk_in_recv, dk_own)

    rs_in[c] = rs_out[c]
    for d in range(1, n_ctx):
        rs_arrival(lax.rem(c + d, n_ctx)).wait_recv()
    tile = rs_in[0]
    for s in range(1, n_ctx):
        tile = tile + rs_in[s]
    ag[c] = tile

    def ag_copy(d):
        return pltpu.make_async_remote_copy(
            src_ref=ag.at[c],
            dst_ref=ag.at[c],
            send_sem=ag_send.at[d],
            recv_sem=ag_recv.at[c],
            device_id={"ctx": lax.rem(c + d, n_ctx)},
            device_id_type=MESH,
        )

    def ag_arrival(s):
        return pltpu.make_async_remote_copy(
            src_ref=ag.at[s],
            dst_ref=ag.at[s],
            send_sem=ag_send.at[0],
            recv_sem=ag_recv.at[s],
            device_id={"ctx": s},
            device_id_type=MESH,
        )

    for d in range(1, n_ctx):
        ag_copy(d).start()

    for d in range(1, n_ctx):
        ag_arrival(lax.rem(c + d, n_ctx)).wait_recv()
    slices = []
    for b in range(HEADS):
        slices.append(jnp.concatenate([ag[b, :RANK, :], ag[HEADS + b, :RANK, :]], axis=0))
    mine[...] = jnp.concatenate(slices, axis=1).astype(BF16)

    def full_copy(d):
        return pltpu.make_async_remote_copy(
            src_ref=mine,
            dst_ref=full.at[t],
            send_sem=full_send.at[d],
            recv_sem=full_recv.at[t],
            device_id={"tp": lax.rem(t + d, n_tp)},
            device_id_type=MESH,
        )

    def full_arrival(s):
        return pltpu.make_async_remote_copy(
            src_ref=mine,
            dst_ref=full.at[s],
            send_sem=full_send.at[0],
            recv_sem=full_recv.at[s],
            device_id={"tp": s},
            device_id_type=MESH,
        )

    for d in range(1, n_tp):
        full_copy(d).start()
    own_share = pltpu.make_async_copy(mine, full.at[t], out_sem.at[3])
    own_share.start()
    for b in range(HEADS + 1):
        gb_ref[:, b * FEATURES : (b + 1) * FEATURES] = ag[b, RANK:, :]
    own_gb = pltpu.make_async_copy(gb_ref, gb_hbm, out_sem.at[4])
    own_gb.start()
    for p in range(PLACES):

        @pl.when(place == p)
        def _(p=p):
            total = dk_own[...]
            for src in range(p + 1, PLACES):
                term_copy(dk_out, dk_send, dk_in_recv, src, p).wait_recv()
                total = total + dk_in[src - 1].astype(F32)
            gk_ref[...] = unrotate(total, pl.ds(0, rows)).astype(BF16)

    pltpu.make_async_copy(gk_ref, gk_hbm, out_sem.at[2]).start()
    for d in range(1, n_tp):
        full_arrival(lax.rem(t + d, n_tp)).wait_recv()

    for d in range(1, n_ctx):
        rs_copy(d).wait_send()
        ag_copy(d).wait_send()
    for d in range(1, n_tp):
        pull_copy(d).wait_send()
        hid_copy(d).wait_send()
        full_copy(d).wait_send()
    for p in range(PLACES):

        @pl.when(place == p)
        def _(p=p):
            for src, dst, send, recv in ((k_hbm, kall, k_send, k_recv), (v_hbm, vall, v_send, v_recv)):
                for i, to in enumerate(DIRECT[p]):
                    send_block(src, dst, p, to, send.at[i], recv).wait_send()
                if p in HANDED:
                    b, to = HANDED[p]
                    send_block(dst.at[block(b)], dst, b, to, send.at[2], recv).wait_send()
            for b in range(p):
                term_copy(dv_out, dv_send, dv_in_recv, p, b).wait_send()
                term_copy(dk_out, dk_send, dk_in_recv, p, b).wait_send()

    pltpu.make_async_copy(dqs, dq_hbm, out_sem.at[0]).wait()
    pltpu.make_async_copy(gv_ref, gv_hbm, out_sem.at[1]).wait()
    pltpu.make_async_copy(gk_ref, gk_hbm, out_sem.at[2]).wait()
    own_share.wait()
    own_gb.wait()


def finish(dq_in, gk_in, gv_in, gb_in, full_in, dq, gk, gv, gaq, gbq, gav, gbv, dq_v, gk_v, gv_v, gb_v, full_v, ga_v, sem, out_sem):
    width = gbq.shape[1]
    rows = dq_in.shape[0]
    part = rows // finish_parts

    def piece(ref, i):
        return ref.at[pl.ds(i * part, part)]

    moves = [(piece(dq_in, i), piece(dq_v, i), piece(dq, i)) for i in range(finish_parts)]
    moves += [(gk_in, gk_v, gk), (gv_in, gv_v, gv)]
    loads = [pltpu.make_async_copy(a, b, sem.at[i]) for i, (a, b, _) in enumerate(moves)]
    stores = [pltpu.make_async_copy(b, c, out_sem.at[i]) for i, (_, b, c) in enumerate(moves)]
    n = len(moves)
    load_full = pltpu.make_async_copy(full_in, full_v, sem.at[n])
    load_gb = pltpu.make_async_copy(gb_in, gb_v, sem.at[n + 1])
    load_full.start()
    for load in loads:
        load.start()
    load_gb.start()
    for s in range(2):
        stores.append(pltpu.make_async_copy(ga_v.at[s], (gaq, gav)[s], out_sem.at[n + s]))
    load_full.wait()
    for s in range(full_in.shape[0]):
        whole = full_v[s].astype(F32)
        ga_v[0, :, s * width : (s + 1) * width] = whole[:RANK]
        ga_v[1, :, s * width : (s + 1) * width] = whole[RANK:]
    stores[n].start()
    stores[n + 1].start()
    for load, store in zip(loads, stores):
        load.wait()
        store.start()
    load_gb.wait()
    stores.append(pltpu.make_async_copy(gb_v.at[:, pl.ds(0, width)], gbq, out_sem.at[n + 2]))
    stores.append(pltpu.make_async_copy(gb_v.at[:, pl.ds(width, FEATURES)], gbv, out_sem.at[n + 3]))
    stores[n + 2].start()
    stores[n + 3].start()
    for store in stores:
        store.wait()


finish_parts = 4


def shards(x, q, k, v, do, positions, down_q, up_q, down_v, up_v):
    n_ctx, n_tp = lax.axis_size("ctx"), lax.axis_size("tp")
    rows = q.shape[0]
    model = x.shape[1]
    keys = PLACES * rows
    halves = rows // CHUNK
    width = HEADS * FEATURES
    any_spec = pl.BlockSpec(memory_space=pl.ANY)
    vmem = pl.BlockSpec(memory_space=pltpu.VMEM)
    dma = pltpu.SemaphoreType.DMA
    terms = pltpu.VMEM((PLACES - 1, rows, FEATURES), BF16)
    whole = pltpu.VMEM((rows, FEATURES), F32)
    results = pl.pallas_call(
        functools.partial(kernel, n_ctx, n_tp, rows),
        out_shape=(
            jax.ShapeDtypeStruct((rows, width), BF16),
            jax.ShapeDtypeStruct((rows, FEATURES), BF16),
            jax.ShapeDtypeStruct((rows, FEATURES), BF16),
            jax.ShapeDtypeStruct((RANK, width + FEATURES), F32),
            jax.ShapeDtypeStruct((n_tp, 2 * RANK, width), BF16),
        ),
        in_specs=[any_spec] * 5 + [vmem] * 5,
        out_specs=(any_spec,) * 5,
        scratch_shapes=[
            pltpu.VMEM((rows, width), BF16),
            pltpu.VMEM((rows // n_tp, model), BF16),
            pltpu.VMEM((keys, FEATURES), BF16),
            pltpu.VMEM((keys, FEATURES), BF16),
            pltpu.VMEM((FEATURES, keys), BF16),
            pltpu.VMEM((FEATURES + 2 * RANK, keys), BF16),
            pltpu.VMEM((halves, HEADS * CHUNK, FEATURES), BF16),
            pltpu.VMEM((halves, HEADS * CHUNK, FEATURES), BF16),
            pltpu.VMEM((halves, keys, HEADS * CHUNK), BF16),
            pltpu.VMEM((halves, keys, CHUNK), F32),
            pltpu.VMEM((halves * HEADS, 1, CHUNK), F32),
            pltpu.VMEM((rows, width), BF16),
            terms,
            terms,
            terms,
            terms,
            whole,
            whole,
            whole,
            whole,
            pltpu.VMEM((2 * RANK, model), BF16),
            pltpu.VMEM((n_tp, rows // n_tp, FEATURES), BF16),
            pltpu.VMEM((n_tp, 2 * RANK, rows), F32),
            pltpu.VMEM((n_ctx, 2 * RANK, FEATURES), F32),
            pltpu.VMEM((n_ctx, 2 * RANK, FEATURES), F32),
            pltpu.VMEM((n_ctx, 2 * RANK, FEATURES), F32),
            pltpu.VMEM((2 * RANK, width), BF16),
            pltpu.VMEM((rows, FEATURES), BF16),
            pltpu.VMEM((rows, FEATURES), BF16),
            pltpu.VMEM((RANK, width + FEATURES), F32),
            dma((2, halves * HEADS)),
            dma((2,)),
            dma((5,)),
            dma((2,)),
            dma((3,)),
            dma((PLACES,)),
            dma((3,)),
            dma((PLACES,)),
            dma((PLACES - 1,)),
            dma((PLACES - 1,)),
            dma((PLACES - 1,)),
            dma((PLACES - 1,)),
            dma((n_tp,)),
            dma((n_tp,)),
            dma((n_ctx,)),
            dma((n_ctx,)),
            dma((n_ctx,)),
            dma((n_ctx,)),
            dma((n_tp,)),
            dma((n_tp,)),
            dma((n_tp,)),
            dma((n_tp,)),
        ],
        compiler_params=pltpu.CompilerParams(
            collective_id=0, has_side_effects=True, vmem_limit_bytes=56 * 1024 * 1024
        ),
        cost_estimate=pl.CostEstimate(flops=12 * 10**9, bytes_accessed=16 * 10**6, transcendentals=8 * 10**6),
    )(x, q, k, v, do, positions.reshape(1, rows), down_q, up_q, down_v, up_v)
    return pl.pallas_call(
        finish,
        out_shape=(
            jax.ShapeDtypeStruct((rows, width), BF16),
            jax.ShapeDtypeStruct((rows, FEATURES), BF16),
            jax.ShapeDtypeStruct((rows, FEATURES), BF16),
            jax.ShapeDtypeStruct((RANK, model), F32),
            jax.ShapeDtypeStruct((RANK, width), F32),
            jax.ShapeDtypeStruct((RANK, model), F32),
            jax.ShapeDtypeStruct((RANK, FEATURES), F32),
        ),
        in_specs=[any_spec] * 5,
        out_specs=(any_spec,) * 7,
        scratch_shapes=[
            pltpu.VMEM((rows, width), BF16),
            pltpu.VMEM((rows, FEATURES), BF16),
            pltpu.VMEM((rows, FEATURES), BF16),
            pltpu.VMEM((RANK, width + FEATURES), F32),
            pltpu.VMEM((n_tp, 2 * RANK, width), BF16),
            pltpu.VMEM((2, RANK, model), F32),
            dma((finish_parts + 4,)),
            dma((finish_parts + 6,)),
        ],
        compiler_params=pltpu.CompilerParams(vmem_limit_bytes=56 * 1024 * 1024),
    )(*results)


def solution(mesh):
    in_specs = (
        P("ctx", None),
        P("ctx", "tp"),
        P("ctx", "tp"),
        P("ctx", "tp"),
        P("ctx", "tp"),
        P("ctx"),
        P(),
        P(None, "tp"),
        P(),
        P(None, "tp"),
    )
    out_specs = (
        P("ctx", "tp"),
        P("ctx", "tp"),
        P("ctx", "tp"),
        P(),
        P(None, "tp"),
        P(),
        P(None, "tp"),
    )
    return jax.shard_map(shards, mesh=mesh, in_specs=in_specs, out_specs=out_specs, check_vma=False)
```

```python
import functools
import math

import jax
import jax.numpy as jnp
from jax import lax
from jax.experimental import pallas as pl
from jax.experimental.pallas import tpu as pltpu
from jax.sharding import PartitionSpec as P

QUERY_HEADS = 64
KEY_VALUE_HEADS = 8
FEATURES = 128
RANK = 8
SCALE_NUM = 1
SCALE_DEN = 8
ROPE_BASE = 10000.0
PLACES = 4
CHUNK = 256
HEADS = QUERY_HEADS // KEY_VALUE_HEADS
SCALE = FEATURES**-0.5
SCALE_LOG2 = SCALE * math.log2(math.e)

F32 = jnp.float32
BF16 = jnp.bfloat16
MESH = pl.DeviceIdType.MESH

SUMMED = {2: (0, 0), 3: (1, 1)}
SOURCES = {0: (1, 2), 1: (3,), 2: (3,), 3: ()}

DIRECT = {0: (1, 2), 1: (3,), 2: (3,), 3: ()}
HANDED = {2: (0, 3), 3: (1, 2)}


def nt(a, b):
    return lax.dot_general(a, b, (((1,), (1,)), ((), ())), preferred_element_type=F32)


def nn(a, b):
    return jnp.dot(a, b, preferred_element_type=F32)


def fold(a, op):
    return op(a.reshape(a.shape[0] // 8, 8, a.shape[1]), axis=0)


def kernel(
    n_ctx,
    n_tp,
    rows,
    x_hbm,
    q_hbm,
    k_hbm,
    v_hbm,
    do_hbm,
    pos_ref,
    dq_down_ref,
    up_q_ref,
    dv_down_ref,
    up_v_ref,
    dq_hbm,
    gk_hbm,
    gv_hbm,
    gb_hbm,
    full_hbm,
    xs,
    xr,
    kall,
    vall,
    ktr,
    vtr,
    qs,
    dos,
    dos_far,
    prob,
    work,
    peaks,
    deltas,
    dqs,
    dv_out,
    dv_in,
    dk_out,
    dk_in,
    dv_own,
    dk_own,
    ctab,
    stab,
    down,
    hid,
    pulls,
    gb_half,
    gb_in,
    gb_sums,
    gb_ref,
    ga_half,
    ga_in,
    ga_sums,
    full,
    gk_ref,
    gv_ref,
    load_sem,
    xsem,
    out_sem,
    own_sem,
    k_send,
    k_recv,
    v_send,
    v_recv,
    dv_send,
    dv_recv,
    dk_send,
    dk_recv,
    pull_send,
    pull_recv,
    sib_send,
    sib_recv,
    gbc_send,
    gbc_recv,
    gac_send,
    gac_recv,
    full_send,
    full_recv,
    hid_send,
    hid_recv,
):
    c = lax.axis_index("ctx")
    t = lax.axis_index("tp")
    halves = rows // CHUNK
    width = HEADS * FEATURES
    shifted = jnp.where(t >= n_tp // 2, PLACES // 2, 0)
    place = lax.rem(c + shifted, PLACES)

    def member(j):
        return lax.rem(c - place + j + n_ctx, n_ctx)

    barrier = pltpu.get_barrier_semaphore()
    core = lax.rem(c, 2)
    sibling = c + 1 - 2 * core
    chips = n_ctx // 2
    for peer in [sibling, member(PLACES - 1 - place)] + [lax.rem(c + 2 * d, n_ctx) for d in range(1, chips)]:
        pl.semaphore_signal(barrier, inc=1, device_id={"ctx": peer}, device_id_type=MESH)
    for d in range(1, n_tp):
        pl.semaphore_signal(barrier, inc=1, device_id={"tp": lax.rem(t + d, n_tp)}, device_id_type=MESH)

    own = pl.ds(pl.multiple_of(place * rows, rows), rows)
    own_k = pltpu.make_async_copy(k_hbm, kall.at[own], own_sem.at[0])
    own_v = pltpu.make_async_copy(v_hbm, vall.at[own], own_sem.at[1])
    own_k.start()
    loads = []
    for j in range(halves):
        for h in range(HEADS):
            for n, (src, dst) in enumerate(((q_hbm, qs), (do_hbm, dos))):
                loads.append(
                    pltpu.make_async_copy(
                        src.at[pl.ds(j * CHUNK, CHUNK), pl.ds(h * FEATURES, FEATURES)],
                        dst.at[j, pl.ds(h * CHUNK, CHUNK)],
                        load_sem.at[n, j * HEADS + h],
                    )
                )
    part = rows // n_tp
    load_rows = pltpu.make_async_copy(x_hbm.at[pl.ds(pl.multiple_of(t * part, part), part)], xr, xsem.at[0])
    load_share = pltpu.make_async_copy(x_hbm.at[:, pl.ds(pl.multiple_of(t * width, width), width)], xs, xsem.at[1])
    load_rows.start()
    for copy in loads:
        copy.start()
    own_v.start()
    load_share.start()

    pl.semaphore_wait(barrier, chips + n_tp)

    def block(b):
        return pl.ds(b * rows, rows)

    def send_block(src, dst, b, to, send, recv):
        return pltpu.make_async_remote_copy(
            src_ref=src,
            dst_ref=dst.at[block(b)],
            send_sem=send,
            recv_sem=recv.at[b],
            device_id={"ctx": member(to)},
            device_id_type=MESH,
        )

    for p in range(PLACES):

        @pl.when(place == p)
        def _(p=p):
            for i, to in enumerate(DIRECT[p]):
                send_block(k_hbm, kall, p, to, k_send.at[i], k_recv).start()

    lane = lax.broadcasted_iota(jnp.int32, (FEATURES, rows), 0)
    index = jnp.where(lane < FEATURES // 2, lane, lane - FEATURES // 2).astype(F32)
    inverse = jnp.exp(index * (-2.0 / FEATURES) * jnp.log(F32(ROPE_BASE)))
    angle = ((pos_ref[...] * SCALE_NUM).astype(F32) / SCALE_DEN) * inverse
    ctab[...] = jnp.cos(angle).T
    stab[...] = jnp.where(lane < FEATURES // 2, jnp.sin(angle), -jnp.sin(angle)).T

    ones = lax.broadcasted_iota(jnp.int32, (2 * RANK, PLACES * rows), 0) == 0
    vtr[FEATURES:, :] = jnp.where(ones, 1.0, 0.0).astype(BF16)
    down[...] = jnp.concatenate([dq_down_ref[...].astype(F32), dv_down_ref[...].astype(F32)], axis=0).astype(BF16)
    load_rows.wait()
    h = nt(xr[...], down[...])
    hid[t] = jnp.concatenate([h, jnp.zeros((part, FEATURES - 2 * RANK), F32)], axis=1).astype(BF16)

    def hid_copy(d):
        return pltpu.make_async_remote_copy(
            src_ref=hid.at[t],
            dst_ref=hid.at[t],
            send_sem=hid_send.at[d],
            recv_sem=hid_recv.at[t],
            device_id={"tp": lax.rem(t + d, n_tp)},
            device_id_type=MESH,
        )

    def hid_arrival(s):
        return pltpu.make_async_remote_copy(
            src_ref=hid.at[s],
            dst_ref=hid.at[s],
            send_sem=hid_send.at[0],
            recv_sem=hid_recv.at[s],
            device_id={"tp": s},
            device_id_type=MESH,
        )

    for d in range(1, n_tp):
        hid_copy(d).start()
    for p in range(PLACES):

        @pl.when(place == p)
        def _(p=p):
            for i, to in enumerate(DIRECT[p]):
                send_block(v_hbm, vall, p, to, v_send.at[i], v_recv).start()

    for copy in loads:
        copy.wait()
    own_k.wait()
    own_v.wait()

    causal = lax.broadcasted_iota(jnp.int32, (CHUNK, CHUNK), 0) <= lax.broadcasted_iota(jnp.int32, (CHUNK, CHUNK), 1)

    def unrotate(a, tokens):
        return a * ctab[tokens, :] + pltpu.roll(a, FEATURES // 2, 1) * stab[tokens, :]

    def attention(p):
        def tiles(j):
            return halves * p + j + 1

        def take(i):
            return pl.ds(i * CHUNK, CHUNK)

        def arrive(dst, send, recv, kind, done=None):
            src = k_hbm if kind == 0 else v_hbm
            if p in HANDED:
                b, to = HANDED[p]
                send_block(src, dst, b, to, send.at[2], recv).wait_recv()
                send_block(dst.at[block(b)], dst, b, to, send.at[2], recv).start()
            for b in range(p):
                if b != done and (p not in HANDED or b != HANDED[p][0]):
                    send_block(src, dst, b, b, send.at[0], recv).wait_recv()

        spans = [(0, 0, 2 * rows), (1, 2 * rows, None)] if p >= 2 else [(1, 0, None)]

        def span(g, j):
            _, a, b = next(s for s in spans if s[0] == g)
            return a, tiles(j) * CHUNK if b is None else b

        def softmax(g):
            @pl.loop(0, HEADS)
            def _(h):
                cols = pl.ds(pl.multiple_of(h * CHUNK, CHUNK), CHUNK)
                for j in range(halves):
                    query = qs[j, cols, :]
                    first, end = span(g, j)
                    last = end - CHUNK if g else end
                    starts = list(range(first, last, 2 * CHUNK)) + [last] * (g == 1)
                    peak = None
                    for a, b in zip(starts, starts[1:] + [end]):
                        s = nt(kall[a:b, :], query)
                        if g and a == last:
                            s = jnp.where(causal, s, -1e30)
                        work[j, a:b, :] = s
                        top = fold(s, jnp.max)
                        peak = top if peak is None else jnp.maximum(peak, top)
                    peak = jnp.max(peak, axis=0, keepdims=True) * SCALE_LOG2
                    peaks[g, j * HEADS + h] = peak
                    for a in range(first, end, CHUNK):
                        b = a + CHUNK
                        prob[j, a:b, cols] = jnp.exp2(work[j, a:b, :] * SCALE_LOG2 - peak).astype(BF16)

        near = {1: 0, 3: 2}
        if p in near:
            send_block(k_hbm, kall, near[p], near[p], k_send.at[0], k_recv).wait_recv()
        softmax(1)
        arrive(kall, k_send, k_recv, 0, near.get(p))
        for i in range(halves * (p + 1)):
            ktr[:, take(i)] = kall[take(i), :].astype(F32).T.astype(BF16)
        if p >= 2:
            softmax(0)

        scaled = (dos_far, dos)
        arrive(vall, v_send, v_recv, 1)
        for i in range(halves * (p + 1)):
            vtr[:FEATURES, take(i)] = vall[take(i), :].astype(F32).T.astype(BF16)

        @pl.loop(0, HEADS)
        def _(h):
            cols = pl.ds(pl.multiple_of(h * CHUNK, CHUNK), CHUNK)
            for j in range(halves):
                u = j * HEADS + h
                outs = {}
                for g, _, _ in spans:
                    a, b = span(g, j)
                    outs[g] = nn(vtr[:, a:b], prob[j, a:b, cols])
                if p >= 2:
                    peak = jnp.maximum(peaks[0, u], peaks[1, u])
                    factor = {g: jnp.exp2(peaks[g, u] - peak) for g in outs}
                    out = outs[0] * factor[0] + outs[1] * factor[1]
                    inv = 1.0 / out[FEATURES : FEATURES + 1]
                    factor = {g: factor[g] * inv for g in outs}
                else:
                    out = outs[1]
                    inv = 1.0 / out[FEATURES : FEATURES + 1]
                    factor = {1: inv}
                up = dos[j, cols, :].astype(F32).T
                delta = jnp.sum(up * out[:FEATURES], axis=0, keepdims=True) * inv
                for g in outs:
                    deltas[g, u] = delta * factor[g]
                    scaled[g][j, cols, :] = (up * factor[g]).T.astype(BF16)

        key_terms(p, range(p), True, (dos_far if p >= 2 else dos, dos), None, dv_out, dv_send, dv_in_recv, dv_own)

        @pl.loop(0, HEADS)
        def _(h):
            cols = pl.ds(pl.multiple_of(h * CHUNK, CHUNK), CHUNK)
            for j in range(halves):
                length = tiles(j) * CHUNK
                for g, _, _ in spans:
                    up = scaled[g][j, cols, :]
                    delta = deltas[g, j * HEADS + h]
                    first, end = span(g, j)
                    for a in range(first, end, 4 * CHUNK):
                        b = min(a + 4 * CHUNK, end)
                        m = nt(vall[a:b, :], up)
                        prob[j, a:b, cols] = (prob[j, a:b, cols].astype(F32) * (m - delta)).astype(BF16)
                grad = nn(ktr[:, :length], prob[j, :length, cols])
                out = unrotate(grad.T * SCALE, take(j))
                dqs[take(j), pl.ds(pl.multiple_of(h * FEATURES, FEATURES), FEATURES)] = out.astype(BF16)

        pltpu.make_async_copy(dqs, dq_hbm, out_sem.at[0]).start()

        total = dv_own[...]
        for src in range(p + 1, PLACES):
            term_copy(dv_out, dv_send, dv_in_recv, src, p).wait_recv()
            total = total + dv_in[src - 1].astype(F32)
        gv_ref[...] = total.astype(BF16)
        pltpu.make_async_copy(gv_ref, gv_hbm, out_sem.at[1]).start()

        pull = jnp.concatenate([nt(up_q_ref[...], dqs[...]), nt(up_v_ref[...], gv_ref[...])], axis=0)
        pulls[t] = pull.astype(BF16)
        for d in range(1, n_tp):
            pull_copy(d).start()

        key_terms(p, range(p), True, (qs, qs), SCALE, dk_out, dk_send, dk_in_recv, dk_own, SUMMED)

    def key_terms(p, blocks, home, right, scale, outs, send, into, kept, summed=()):
        def finish(a):
            return a if scale is None else a * scale

        for b in blocks:
            r = right[b // 2]
            a = nn(prob[0, block(b), :], r[0])
            for j in range(1, halves):
                a = a + nn(prob[j, block(b), :], r[j])
            outs[b] = finish(a).astype(BF16)
            if p not in summed or b != summed[p][0]:
                term_copy(outs, send, into, p, b, summed).start()
        if home:
            for i in range(halves):
                a = None
                for j in range(i, halves):
                    m = nn(prob[j, pl.ds((halves * p + i) * CHUNK, CHUNK), :], right[1][j])
                    a = m if a is None else a + m
                kept[pl.ds(i * CHUNK, CHUNK), :] = finish(a)

    dv_in_recv = (dv_in, dv_recv)
    dk_in_recv = (dk_in, dk_recv)

    def term_copy(outs, send, into, src, b, summed=()):
        dst, recv = into
        to, slot = b, src - 1
        if src in summed and b == summed[5 - src][0]:
            to, slot = 5 - src, summed[5 - src][1]
        return pltpu.make_async_remote_copy(
            src_ref=outs.at[b],
            dst_ref=dst.at[slot],
            send_sem=send.at[b],
            recv_sem=recv.at[slot],
            device_id={"ctx": member(to)},
            device_id_type=MESH,
        )

    def pull_copy(d):
        return pltpu.make_async_remote_copy(
            src_ref=pulls.at[t],
            dst_ref=pulls.at[t],
            send_sem=pull_send.at[d],
            recv_sem=pull_recv.at[t],
            device_id={"tp": lax.rem(t + d, n_tp)},
            device_id_type=MESH,
        )

    def pull_arrival(s):
        return pltpu.make_async_remote_copy(
            src_ref=pulls.at[s],
            dst_ref=pulls.at[s],
            send_sem=pull_send.at[0],
            recv_sem=pull_recv.at[s],
            device_id={"tp": s},
            device_id_type=MESH,
        )

    for p in range(PLACES):
        pl.when(place == p)(functools.partial(attention, p))

    for d in range(1, n_tp):
        hid_arrival(lax.rem(t + d, n_tp)).wait_recv()
    hidden = hid[...].astype(F32).reshape(rows, FEATURES).T[: 2 * RANK].astype(BF16)
    gb = nn(hidden, dqs[...])[:RANK]
    gbv = nn(hidden, gv_ref[...])[RANK:]
    half = width // 2
    for i in range(2):
        gb_half[i, :, :half] = gb[:, i * half : (i + 1) * half]
        gb_half[i, :, half:] = gbv

    def to_sibling(src, dst, n):
        return pltpu.make_async_remote_copy(
            src_ref=src,
            dst_ref=dst,
            send_sem=sib_send.at[n],
            recv_sem=sib_recv.at[n],
            device_id={"ctx": sibling},
            device_id_type=MESH,
        )

    gb_pair = to_sibling(gb_half.at[1 - core], gb_in, 0)
    gb_pair.start()

    for d in range(1, n_tp):
        pull_arrival(lax.rem(t + d, n_tp)).wait_recv()
    pull = pulls[0].astype(F32)
    for s in range(1, n_tp):
        pull = pull + pulls[s].astype(F32)
    high = pull.astype(BF16)
    low = (pull - high.astype(F32)).astype(BF16)
    load_share.wait()
    ga = nn(high, xs[...]) + nn(low, xs[...])
    for i in range(2):
        ga_half[i] = ga[:, i * half : (i + 1) * half]
    ga_pair = to_sibling(ga_half.at[1 - core], ga_in, 1)
    ga_pair.start()

    chip = c // 2

    def chip_copy(buf, send, recv, d):
        return pltpu.make_async_remote_copy(
            src_ref=buf.at[chip],
            dst_ref=buf.at[chip],
            send_sem=send.at[d],
            recv_sem=recv.at[chip],
            device_id={"ctx": lax.rem(c + 2 * d, n_ctx)},
            device_id_type=MESH,
        )

    def chip_arrival(buf, send, recv, d):
        other = lax.rem(chip + d, chips)
        return pltpu.make_async_remote_copy(
            src_ref=buf.at[other],
            dst_ref=buf.at[other],
            send_sem=send.at[0],
            recv_sem=recv.at[other],
            device_id={"ctx": lax.rem(c + 2 * d, n_ctx)},
            device_id_type=MESH,
        )

    gb_pair.wait_recv()
    gb_sums[chip] = gb_half[core] + gb_in[...]
    for d in range(1, chips):
        chip_copy(gb_sums, gbc_send, gbc_recv, d).start()
    ga_pair.wait_recv()
    ga_sums[chip] = (ga_half[core] + ga_in[...]).astype(BF16)
    for d in range(1, chips):
        chip_copy(ga_sums, gac_send, gac_recv, d).start()

    for d in range(1, chips):
        chip_arrival(ga_sums, gac_send, gac_recv, d).wait_recv()
    total = ga_sums[0].astype(F32)
    for i in range(1, chips):
        total = total + ga_sums[i].astype(F32)
    full[core, t] = total.astype(BF16)

    def full_copy(d):
        return pltpu.make_async_remote_copy(
            src_ref=full.at[core, t],
            dst_ref=full.at[core, t],
            send_sem=full_send.at[d],
            recv_sem=full_recv.at[t],
            device_id={"tp": lax.rem(t + d, n_tp)},
            device_id_type=MESH,
        )

    def full_arrival(s):
        return pltpu.make_async_remote_copy(
            src_ref=full.at[core, s],
            dst_ref=full.at[core, s],
            send_sem=full_send.at[0],
            recv_sem=full_recv.at[s],
            device_id={"tp": s},
            device_id_type=MESH,
        )

    for d in range(1, n_tp):
        full_copy(d).start()

    for p in range(PLACES):

        @pl.when(place == p)
        def _(p=p):
            if p in SUMMED:
                b, slot = SUMMED[p]
                term_copy(dk_out, dk_send, dk_in_recv, 5 - p, b, SUMMED).wait_recv()
                dk_out[b] = (dk_out[b].astype(F32) + dk_in[slot].astype(F32)).astype(BF16)
                term_copy(dk_out, dk_send, dk_in_recv, p, b, SUMMED).start()

    for d in range(1, chips):
        chip_arrival(gb_sums, gbc_send, gbc_recv, d).wait_recv()
    gb = gb_sums[0]
    for i in range(1, chips):
        gb = gb + gb_sums[i]
    gb_ref[core] = gb
    gb_other = to_sibling(gb_ref.at[core], gb_ref.at[core], 2)
    gb_other.start()

    gb_other.wait_recv()
    own_gb = pltpu.make_async_copy(gb_ref, gb_hbm, out_sem.at[4])
    own_gb.start()

    for d in range(1, n_tp):
        full_arrival(lax.rem(t + d, n_tp)).wait_recv()
    full_pair = to_sibling(full.at[core], full.at[core], 3)
    full_pair.start()
    own_share = pltpu.make_async_copy(full.at[core], full_hbm.at[core], out_sem.at[3])
    own_share.start()
    for p in range(PLACES):

        @pl.when(place == p)
        def _(p=p):
            total = dk_own[...]
            for src in SOURCES[p]:
                term_copy(dk_out, dk_send, dk_in_recv, src, p, SUMMED).wait_recv()
                total = total + dk_in[src - 1].astype(F32)
            gk_ref[...] = unrotate(total, pl.ds(0, rows)).astype(BF16)

    pltpu.make_async_copy(gk_ref, gk_hbm, out_sem.at[2]).start()
    full_pair.wait_recv()
    other_share = pltpu.make_async_copy(full.at[1 - core], full_hbm.at[1 - core], out_sem.at[5])
    other_share.start()

    for d in range(1, chips):
        chip_copy(gb_sums, gbc_send, gbc_recv, d).wait_send()
        chip_copy(ga_sums, gac_send, gac_recv, d).wait_send()
    for copy in (gb_pair, ga_pair, gb_other, full_pair):
        copy.wait_send()
    for d in range(1, n_tp):
        pull_copy(d).wait_send()
        hid_copy(d).wait_send()
        full_copy(d).wait_send()
    for p in range(PLACES):

        @pl.when(place == p)
        def _(p=p):
            for src, dst, send, recv in ((k_hbm, kall, k_send, k_recv), (v_hbm, vall, v_send, v_recv)):
                for i, to in enumerate(DIRECT[p]):
                    send_block(src, dst, p, to, send.at[i], recv).wait_send()
                if p in HANDED:
                    b, to = HANDED[p]
                    send_block(dst.at[block(b)], dst, b, to, send.at[2], recv).wait_send()
            for b in range(p):
                term_copy(dv_out, dv_send, dv_in_recv, p, b).wait_send()
                term_copy(dk_out, dk_send, dk_in_recv, p, b, SUMMED).wait_send()

    pltpu.make_async_copy(dqs, dq_hbm, out_sem.at[0]).wait()
    pltpu.make_async_copy(gv_ref, gv_hbm, out_sem.at[1]).wait()
    pltpu.make_async_copy(gk_ref, gk_hbm, out_sem.at[2]).wait()
    own_share.wait()
    other_share.wait()
    own_gb.wait()


def finish(dq_in, gk_in, gv_in, gb_in, full_in, dq, gk, gv, gaq, gbq, gav, gbv, dq_v, gk_v, gv_v, gb_v, full_v, ga_v, sem, out_sem):
    width = gbq.shape[1]
    rows = dq_in.shape[0]
    part = rows // finish_parts

    def piece(ref, i):
        return ref.at[pl.ds(i * part, part)]

    moves = [(piece(dq_in, i), piece(dq_v, i), piece(dq, i)) for i in range(finish_parts)]
    moves += [(gk_in, gk_v, gk), (gv_in, gv_v, gv)]
    loads = [pltpu.make_async_copy(a, b, sem.at[i]) for i, (a, b, _) in enumerate(moves)]
    stores = [pltpu.make_async_copy(b, c, out_sem.at[i]) for i, (_, b, c) in enumerate(moves)]
    n = len(moves)
    load_full = pltpu.make_async_copy(full_in, full_v, sem.at[n])
    load_gb = pltpu.make_async_copy(gb_in, gb_v, sem.at[n + 1])
    load_full.start()
    for load in loads:
        load.start()
    load_gb.start()
    for s in range(2):
        stores.append(pltpu.make_async_copy(ga_v.at[s], (gaq, gav)[s], out_sem.at[n + s]))
    load_full.wait()
    half = width // 2
    for s in range(full_in.shape[1]):
        for i in range(2):
            whole = full_v[i, s].astype(F32)
            a = s * width + i * half
            ga_v[0, :, a : a + half] = whole[:RANK]
            ga_v[1, :, a : a + half] = whole[RANK:]
    stores[n].start()
    stores[n + 1].start()
    for load, store in zip(loads, stores):
        load.wait()
        store.start()
    load_gb.wait()
    for i in range(2):
        stores.append(pltpu.make_async_copy(gb_v.at[i, :, pl.ds(0, half)], gbq.at[:, pl.ds(i * half, half)], out_sem.at[n + 2 + i]))
    stores.append(pltpu.make_async_copy(gb_v.at[0, :, pl.ds(half, FEATURES)], gbv, out_sem.at[n + 4]))
    for store in stores[n + 2 :]:
        store.start()
    for store in stores:
        store.wait()


finish_parts = 4


def shards(x, q, k, v, do, positions, down_q, up_q, down_v, up_v):
    n_ctx, n_tp = lax.axis_size("ctx"), lax.axis_size("tp")
    rows = q.shape[0]
    model = x.shape[1]
    keys = PLACES * rows
    halves = rows // CHUNK
    width = HEADS * FEATURES
    any_spec = pl.BlockSpec(memory_space=pl.ANY)
    vmem = pl.BlockSpec(memory_space=pltpu.VMEM)
    dma = pltpu.SemaphoreType.DMA
    terms = pltpu.VMEM((PLACES - 1, rows, FEATURES), BF16)
    whole = pltpu.VMEM((rows, FEATURES), F32)
    results = pl.pallas_call(
        functools.partial(kernel, n_ctx, n_tp, rows),
        out_shape=(
            jax.ShapeDtypeStruct((rows, width), BF16),
            jax.ShapeDtypeStruct((rows, FEATURES), BF16),
            jax.ShapeDtypeStruct((rows, FEATURES), BF16),
            jax.ShapeDtypeStruct((2, RANK, width // 2 + FEATURES), F32),
            jax.ShapeDtypeStruct((2, n_tp, 2 * RANK, width // 2), BF16),
        ),
        in_specs=[any_spec] * 5 + [vmem] * 5,
        out_specs=(any_spec,) * 5,
        scratch_shapes=[
            pltpu.VMEM((rows, width), BF16),
            pltpu.VMEM((rows // n_tp, model), BF16),
            pltpu.VMEM((keys, FEATURES), BF16),
            pltpu.VMEM((keys, FEATURES), BF16),
            pltpu.VMEM((FEATURES, keys), BF16),
            pltpu.VMEM((FEATURES + 2 * RANK, keys), BF16),
            pltpu.VMEM((halves, HEADS * CHUNK, FEATURES), BF16),
            pltpu.VMEM((halves, HEADS * CHUNK, FEATURES), BF16),
            pltpu.VMEM((halves, HEADS * CHUNK, FEATURES), BF16),
            pltpu.VMEM((halves, keys, HEADS * CHUNK), BF16),
            pltpu.VMEM((halves, keys, CHUNK), F32),
            pltpu.VMEM((2, halves * HEADS, 1, CHUNK), F32),
            pltpu.VMEM((2, halves * HEADS, 1, CHUNK), F32),
            pltpu.VMEM((rows, width), BF16),
            terms,
            terms,
            terms,
            terms,
            whole,
            whole,
            whole,
            whole,
            pltpu.VMEM((2 * RANK, model), BF16),
            pltpu.VMEM((n_tp, rows // n_tp, FEATURES), BF16),
            pltpu.VMEM((n_tp, 2 * RANK, rows), BF16),
            pltpu.VMEM((2, RANK, width // 2 + FEATURES), F32),
            pltpu.VMEM((RANK, width // 2 + FEATURES), F32),
            pltpu.VMEM((n_ctx // 2, RANK, width // 2 + FEATURES), F32),
            pltpu.VMEM((2, RANK, width // 2 + FEATURES), F32),
            pltpu.VMEM((2, 2 * RANK, width // 2), F32),
            pltpu.VMEM((2 * RANK, width // 2), F32),
            pltpu.VMEM((n_ctx // 2, 2 * RANK, width // 2), BF16),
            pltpu.VMEM((2, n_tp, 2 * RANK, width // 2), BF16),
            pltpu.VMEM((rows, FEATURES), BF16),
            pltpu.VMEM((rows, FEATURES), BF16),
            dma((2, halves * HEADS)),
            dma((2,)),
            dma((6,)),
            dma((2,)),
            dma((3,)),
            dma((PLACES,)),
            dma((3,)),
            dma((PLACES,)),
            dma((PLACES - 1,)),
            dma((PLACES - 1,)),
            dma((PLACES - 1,)),
            dma((PLACES - 1,)),
            dma((n_tp,)),
            dma((n_tp,)),
            dma((4,)),
            dma((4,)),
            dma((n_ctx // 2,)),
            dma((n_ctx // 2,)),
            dma((n_ctx // 2,)),
            dma((n_ctx // 2,)),
            dma((n_tp,)),
            dma((n_tp,)),
            dma((n_tp,)),
            dma((n_tp,)),
        ],
        compiler_params=pltpu.CompilerParams(
            collective_id=0, has_side_effects=True, vmem_limit_bytes=56 * 1024 * 1024
        ),
        cost_estimate=pl.CostEstimate(flops=12 * 10**9, bytes_accessed=16 * 10**6, transcendentals=8 * 10**6),
    )(x, q, k, v, do, positions.reshape(1, rows), down_q, up_q, down_v, up_v)
    return pl.pallas_call(
        finish,
        out_shape=(
            jax.ShapeDtypeStruct((rows, width), BF16),
            jax.ShapeDtypeStruct((rows, FEATURES), BF16),
            jax.ShapeDtypeStruct((rows, FEATURES), BF16),
            jax.ShapeDtypeStruct((RANK, model), F32),
            jax.ShapeDtypeStruct((RANK, width), F32),
            jax.ShapeDtypeStruct((RANK, model), F32),
            jax.ShapeDtypeStruct((RANK, FEATURES), F32),
        ),
        in_specs=[any_spec] * 5,
        out_specs=(any_spec,) * 7,
        scratch_shapes=[
            pltpu.VMEM((rows, width), BF16),
            pltpu.VMEM((rows, FEATURES), BF16),
            pltpu.VMEM((rows, FEATURES), BF16),
            pltpu.VMEM((2, RANK, width // 2 + FEATURES), F32),
            pltpu.VMEM((2, n_tp, 2 * RANK, width // 2), BF16),
            pltpu.VMEM((2, RANK, model), F32),
            dma((finish_parts + 4,)),
            dma((finish_parts + 7,)),
        ],
        compiler_params=pltpu.CompilerParams(vmem_limit_bytes=56 * 1024 * 1024),
    )(*results)


def solution(mesh):
    in_specs = (
        P("ctx", None),
        P("ctx", "tp"),
        P("ctx", "tp"),
        P("ctx", "tp"),
        P("ctx", "tp"),
        P("ctx"),
        P(),
        P(None, "tp"),
        P(),
        P(None, "tp"),
    )
    out_specs = (
        P("ctx", "tp"),
        P("ctx", "tp"),
        P("ctx", "tp"),
        P(),
        P(None, "tp"),
        P(),
        P(None, "tp"),
    )
    return jax.shard_map(shards, mesh=mesh, in_specs=in_specs, out_specs=out_specs, check_vma=False)
```

```python
import functools
import math

import jax
import jax.numpy as jnp
from jax import lax
from jax.experimental import pallas as pl
from jax.experimental.pallas import tpu as pltpu
from jax.sharding import PartitionSpec as P

QUERY_HEADS = 64
KEY_VALUE_HEADS = 8
FEATURES = 128
RANK = 8
SCALE_NUM = 1
SCALE_DEN = 8
ROPE_BASE = 10000.0
PLACES = 4
CHUNK = 256
HEADS = QUERY_HEADS // KEY_VALUE_HEADS
SCALE = FEATURES**-0.5
SCALE_LOG2 = SCALE * math.log2(math.e)

F32 = jnp.float32
BF16 = jnp.bfloat16
MESH = pl.DeviceIdType.MESH

SUMMED = {2: (0, 0), 3: (1, 1)}
SOURCES = {0: (1, 2), 1: (3,), 2: (3,), 3: ()}

DIRECT = {0: (1, 2), 1: (3,), 2: (3,), 3: ()}
HANDED = {2: (0, 3), 3: (1, 2)}


def nt(a, b):
    return lax.dot_general(a, b, (((1,), (1,)), ((), ())), preferred_element_type=F32)


def nn(a, b):
    return jnp.dot(a, b, preferred_element_type=F32)


def fold(a, op):
    return op(a.reshape(a.shape[0] // 8, 8, a.shape[1]), axis=0)


def kernel(
    n_ctx,
    n_tp,
    rows,
    x_hbm,
    q_hbm,
    k_hbm,
    v_hbm,
    do_hbm,
    pos_ref,
    dq_down_ref,
    up_q_ref,
    dv_down_ref,
    up_v_ref,
    dq_hbm,
    gk_hbm,
    gv_hbm,
    gb_hbm,
    full_hbm,
    xs,
    xr,
    kall,
    vall,
    ktr,
    vtr,
    qs,
    dos,
    prob,
    work,
    peaks,
    deltas,
    dqs,
    dv_out,
    dv_in,
    dk_out,
    dk_in,
    dv_own,
    dk_own,
    ctab,
    stab,
    down,
    hid,
    pulls,
    gb_half,
    gb_in,
    gb_sums,
    gb_ref,
    ga_half,
    ga_in,
    ga_sums,
    full,
    gk_ref,
    gv_ref,
    load_sem,
    xsem,
    out_sem,
    own_sem,
    k_send,
    k_recv,
    v_send,
    v_recv,
    dv_send,
    dv_recv,
    dk_send,
    dk_recv,
    pull_send,
    pull_recv,
    sib_send,
    sib_recv,
    gbc_send,
    gbc_recv,
    gac_send,
    gac_recv,
    full_send,
    full_recv,
    hid_send,
    hid_recv,
):
    c = lax.axis_index("ctx")
    t = lax.axis_index("tp")
    halves = rows // CHUNK
    width = HEADS * FEATURES
    shifted = jnp.where(t >= n_tp // 2, PLACES // 2, 0)
    place = lax.rem(c + shifted, PLACES)

    def member(j):
        return lax.rem(c - place + j + n_ctx, n_ctx)

    barrier = pltpu.get_barrier_semaphore()
    core = lax.rem(c, 2)
    sibling = c + 1 - 2 * core
    chips = n_ctx // 2
    for peer in [sibling, member(PLACES - 1 - place)] + [lax.rem(c + 2 * d, n_ctx) for d in range(1, chips)]:
        pl.semaphore_signal(barrier, inc=1, device_id={"ctx": peer}, device_id_type=MESH)
    for d in range(1, n_tp):
        pl.semaphore_signal(barrier, inc=1, device_id={"tp": lax.rem(t + d, n_tp)}, device_id_type=MESH)

    own = pl.ds(pl.multiple_of(place * rows, rows), rows)
    own_k = pltpu.make_async_copy(k_hbm, kall.at[own], own_sem.at[0])
    own_v = pltpu.make_async_copy(v_hbm, vall.at[own], own_sem.at[1])
    own_k.start()
    loads = []
    for j in range(halves):
        for h in range(HEADS):
            for n, (src, dst) in enumerate(((q_hbm, qs), (do_hbm, dos.at[1]))):
                loads.append(
                    pltpu.make_async_copy(
                        src.at[pl.ds(j * CHUNK, CHUNK), pl.ds(h * FEATURES, FEATURES)],
                        dst.at[j, pl.ds(h * CHUNK, CHUNK)],
                        load_sem.at[n, j * HEADS + h],
                    )
                )
    part = rows // n_tp
    load_rows = pltpu.make_async_copy(x_hbm.at[pl.ds(pl.multiple_of(t * part, part), part)], xr, xsem.at[0])
    load_share = pltpu.make_async_copy(x_hbm.at[:, pl.ds(pl.multiple_of(t * width, width), width)], xs, xsem.at[1])
    load_rows.start()
    for copy in loads:
        copy.start()
    own_v.start()
    load_share.start()

    pl.semaphore_wait(barrier, chips + n_tp)

    def block(b):
        return pl.ds(b * rows, rows)

    def send_block(src, dst, b, to, send, recv):
        return pltpu.make_async_remote_copy(
            src_ref=src,
            dst_ref=dst.at[block(b)],
            send_sem=send,
            recv_sem=recv.at[b],
            device_id={"ctx": member(to)},
            device_id_type=MESH,
        )

    for p in range(PLACES):

        @pl.when(place == p)
        def _(p=p):
            for i, to in enumerate(DIRECT[p]):
                send_block(k_hbm, kall, p, to, k_send.at[i], k_recv).start()

    index = lax.broadcasted_iota(jnp.int32, (FEATURES // 2, rows), 0).astype(F32)
    inverse = jnp.exp(index * (-2.0 / FEATURES) * jnp.log(F32(ROPE_BASE)))
    angle = ((pos_ref[...] * SCALE_NUM).astype(F32) / SCALE_DEN) * inverse
    cosine, sine = jnp.cos(angle), jnp.sin(angle)
    ctab[...] = jnp.concatenate([cosine, cosine], axis=0).T
    stab[...] = jnp.concatenate([sine, -sine], axis=0).T

    ones = lax.broadcasted_iota(jnp.int32, (2 * RANK, PLACES * rows), 0) == 0
    vtr[FEATURES:, :] = jnp.where(ones, 1.0, 0.0).astype(BF16)
    down[...] = jnp.concatenate([dq_down_ref[...].astype(F32), dv_down_ref[...].astype(F32)], axis=0).astype(BF16)
    load_rows.wait()
    h = nt(xr[...], down[...])
    hid[t] = jnp.concatenate([h, jnp.zeros((part, FEATURES - 2 * RANK), F32)], axis=1).astype(BF16)

    def hid_copy(d):
        return pltpu.make_async_remote_copy(
            src_ref=hid.at[t],
            dst_ref=hid.at[t],
            send_sem=hid_send.at[d],
            recv_sem=hid_recv.at[t],
            device_id={"tp": lax.rem(t + d, n_tp)},
            device_id_type=MESH,
        )

    def hid_arrival(s):
        return pltpu.make_async_remote_copy(
            src_ref=hid.at[s],
            dst_ref=hid.at[s],
            send_sem=hid_send.at[0],
            recv_sem=hid_recv.at[s],
            device_id={"tp": s},
            device_id_type=MESH,
        )

    for d in range(1, n_tp):
        hid_copy(d).start()
    for p in range(PLACES):

        @pl.when(place == p)
        def _(p=p):
            for i, to in enumerate(DIRECT[p]):
                send_block(v_hbm, vall, p, to, v_send.at[i], v_recv).start()

    for copy in loads:
        copy.wait()
    own_k.wait()
    own_v.wait()

    causal = lax.broadcasted_iota(jnp.int32, (CHUNK, CHUNK), 0) <= lax.broadcasted_iota(jnp.int32, (CHUNK, CHUNK), 1)

    def unrotate(a, tokens):
        return a * ctab[tokens, :] + pltpu.roll(a, FEATURES // 2, 1) * stab[tokens, :]

    def spans_of(p):
        spans = [(0, 0, 2 * rows), (1, 2 * rows, None)] if p >= 2 else [(1, 0, None)]

        def span(g, j):
            _, a, b = next(s for s in spans if s[0] == g)
            return a, (halves * p + j + 1) * CHUNK if b is None else b

        return spans, span

    def attention(p):
        def tiles(j):
            return halves * p + j + 1

        def take(i):
            return pl.ds(i * CHUNK, CHUNK)

        def arrive(dst, send, recv, kind, done=None):
            src = k_hbm if kind == 0 else v_hbm
            if p in HANDED:
                b, to = HANDED[p]
                send_block(src, dst, b, to, send.at[2], recv).wait_recv()
                send_block(dst.at[block(b)], dst, b, to, send.at[2], recv).start()
            for b in range(p):
                if b != done and (p not in HANDED or b != HANDED[p][0]):
                    send_block(src, dst, b, b, send.at[0], recv).wait_recv()

        spans, span = spans_of(p)

        def softmax(g):
            @pl.loop(0, HEADS)
            def _(h):
                cols = pl.ds(pl.multiple_of(h * CHUNK, CHUNK), CHUNK)
                for j in range(halves):
                    query = qs[j, cols, :]
                    first, end = span(g, j)
                    last = end - CHUNK if g else end
                    starts = list(range(first, last, 2 * CHUNK)) + [last] * (g == 1)
                    peak = None
                    for a, b in zip(starts, starts[1:] + [end]):
                        s = nt(kall[a:b, :], query)
                        if g and a == last:
                            s = jnp.where(causal, s, -1e30)
                        work[j, a:b, :] = s
                        top = fold(s, jnp.max)
                        peak = top if peak is None else jnp.maximum(peak, top)
                    peak = jnp.max(peak, axis=0, keepdims=True) * SCALE_LOG2
                    peaks[g, j * HEADS + h] = peak
                    for a in range(first, end, CHUNK):
                        b = a + CHUNK
                        prob[j, a:b, cols] = jnp.exp2(work[j, a:b, :] * SCALE_LOG2 - peak).astype(BF16)

        near = {1: 0, 3: 2}
        if p in near:
            send_block(k_hbm, kall, near[p], near[p], k_send.at[0], k_recv).wait_recv()
        softmax(1)
        arrive(kall, k_send, k_recv, 0, near.get(p))
        for i in range(halves * (p + 1)):
            ktr[:, take(i)] = kall[take(i), :].T
        if p >= 2:
            softmax(0)

        arrive(vall, v_send, v_recv, 1)
        for i in range(halves * (p + 1)):
            vtr[:FEATURES, take(i)] = vall[take(i), :].T

        @pl.loop(0, HEADS)
        def _(h):
            cols = pl.ds(pl.multiple_of(h * CHUNK, CHUNK), CHUNK)
            for j in range(halves):
                u = j * HEADS + h
                outs = {}
                for g, _, _ in spans:
                    a, b = span(g, j)
                    outs[g] = nn(vtr[:, a:b], prob[j, a:b, cols])
                if p >= 2:
                    peak = jnp.maximum(peaks[0, u], peaks[1, u])
                    factor = {g: jnp.exp2(peaks[g, u] - peak) for g in outs}
                    out = outs[0] * factor[0] + outs[1] * factor[1]
                    inv = 1.0 / out[FEATURES : FEATURES + 1]
                    factor = {g: factor[g] * inv for g in outs}
                else:
                    out = outs[1]
                    inv = 1.0 / out[FEATURES : FEATURES + 1]
                    factor = {1: inv}
                up = dos[1, j, cols, :].T.astype(F32)
                delta = jnp.sum(up * out[:FEATURES], axis=0, keepdims=True) * inv
                for g in outs:
                    deltas[g, u] = delta * factor[g]
                    dos[g, j, cols, :] = (up * factor[g]).astype(BF16).T

    def query_terms(p):
        def tiles(j):
            return halves * p + j + 1

        def take(i):
            return pl.ds(i * CHUNK, CHUNK)

        spans, span = spans_of(p)

        @pl.loop(0, HEADS)
        def _(h):
            cols = pl.ds(pl.multiple_of(h * CHUNK, CHUNK), CHUNK)
            for j in range(halves):
                length = tiles(j) * CHUNK
                for g, _, _ in spans:
                    up = dos[g, j, cols, :]
                    delta = deltas[g, j * HEADS + h]
                    first, end = span(g, j)
                    for a in range(first, end, 4 * CHUNK):
                        b = min(a + 4 * CHUNK, end)
                        m = nt(vall[a:b, :], up)
                        prob[j, a:b, cols] = (prob[j, a:b, cols].astype(F32) * (m - delta)).astype(BF16)
                grad = nn(ktr[:, :length], prob[j, :length, cols])
                out = unrotate(grad.T * SCALE, take(j))
                dqs[take(j), pl.ds(pl.multiple_of(h * FEATURES, FEATURES), FEATURES)] = out.astype(BF16)

    def key_terms(right, scale, outs, send, into, kept, summed):
        def finish(a):
            return a if scale is None else a * scale

        def product(first, length, j, g):
            return nn(prob[j, pl.ds(pl.multiple_of(first, CHUNK), length), :], right(j, g))

        def other(b, carry):
            g = jnp.where((place >= 2) & (b < 2), 0, 1)
            a = product(b * rows, rows, 0, g)
            for j in range(1, halves):
                a = a + product(b * rows, rows, j, g)
            outs[b] = finish(a).astype(BF16)
            dst, recv = into
            held = place < 0
            to, slot = b, place - 1
            if summed:
                cross = (place >= 2) & (b < 2)
                held = cross & (b == place - 2)
                to, slot = jnp.where(cross, 5 - place, b), jnp.where(cross, b, place - 1)

            @pl.when(jnp.logical_not(held))
            def _():
                pltpu.make_async_remote_copy(
                    src_ref=outs.at[b],
                    dst_ref=dst.at[slot],
                    send_sem=send.at[b],
                    recv_sem=recv.at[slot],
                    device_id={"ctx": member(to)},
                    device_id_type=MESH,
                ).start()

            return carry

        lax.fori_loop(0, place, other, 0)
        for i in range(halves):
            a = None
            for j in range(i, halves):
                m = product(place * rows + i * CHUNK, CHUNK, j, 1)
                a = m if a is None else a + m
            kept[pl.ds(i * CHUNK, CHUNK), :] = finish(a)

    dv_in_recv = (dv_in, dv_recv)
    dk_in_recv = (dk_in, dk_recv)

    def term_copy(outs, send, into, src, b, summed=()):
        dst, recv = into
        to, slot = b, src - 1
        if src in summed and b == summed[5 - src][0]:
            to, slot = 5 - src, summed[5 - src][1]
        return pltpu.make_async_remote_copy(
            src_ref=outs.at[b],
            dst_ref=dst.at[slot],
            send_sem=send.at[b],
            recv_sem=recv.at[slot],
            device_id={"ctx": member(to)},
            device_id_type=MESH,
        )

    def pull_copy(d):
        return pltpu.make_async_remote_copy(
            src_ref=pulls.at[t],
            dst_ref=pulls.at[t],
            send_sem=pull_send.at[d],
            recv_sem=pull_recv.at[t],
            device_id={"tp": lax.rem(t + d, n_tp)},
            device_id_type=MESH,
        )

    def pull_arrival(s):
        return pltpu.make_async_remote_copy(
            src_ref=pulls.at[s],
            dst_ref=pulls.at[s],
            send_sem=pull_send.at[0],
            recv_sem=pull_recv.at[s],
            device_id={"tp": s},
            device_id_type=MESH,
        )

    for p in range(PLACES):
        pl.when(place == p)(functools.partial(attention, p))
    key_terms(lambda j, g: dos[g, j], None, dv_out, dv_send, dv_in_recv, dv_own, False)
    for p in range(PLACES):
        pl.when(place == p)(functools.partial(query_terms, p))
    pltpu.make_async_copy(dqs, dq_hbm, out_sem.at[0]).start()

    for p in range(PLACES):

        @pl.when(place == p)
        def _(p=p):
            total = dv_own[...]
            for src in range(p + 1, PLACES):
                term_copy(dv_out, dv_send, dv_in_recv, src, p).wait_recv()
                total = total + dv_in[src - 1].astype(F32)
            gv_ref[...] = total.astype(BF16)

    pltpu.make_async_copy(gv_ref, gv_hbm, out_sem.at[1]).start()

    pull = jnp.concatenate([nt(up_q_ref[...], dqs[...]), nt(up_v_ref[...], gv_ref[...])], axis=0)
    pulls[t] = pull.astype(BF16)
    for d in range(1, n_tp):
        pull_copy(d).start()

    key_terms(lambda j, g: qs[j], SCALE, dk_out, dk_send, dk_in_recv, dk_own, True)

    for d in range(1, n_tp):
        hid_arrival(lax.rem(t + d, n_tp)).wait_recv()
    hidden = hid[...].astype(F32).reshape(rows, FEATURES).T[: 2 * RANK].astype(BF16)
    gb = nn(hidden, dqs[...])[:RANK]
    gbv = nn(hidden, gv_ref[...])[RANK:]
    half = width // 2
    for i in range(2):
        gb_half[i, :, :half] = gb[:, i * half : (i + 1) * half]
        gb_half[i, :, half:] = gbv

    def to_sibling(src, dst, n):
        return pltpu.make_async_remote_copy(
            src_ref=src,
            dst_ref=dst,
            send_sem=sib_send.at[n],
            recv_sem=sib_recv.at[n],
            device_id={"ctx": sibling},
            device_id_type=MESH,
        )

    gb_pair = to_sibling(gb_half.at[1 - core], gb_in, 0)
    gb_pair.start()

    for d in range(1, n_tp):
        pull_arrival(lax.rem(t + d, n_tp)).wait_recv()
    pull = pulls[0].astype(F32)
    for s in range(1, n_tp):
        pull = pull + pulls[s].astype(F32)
    high = pull.astype(BF16)
    low = (pull - high.astype(F32)).astype(BF16)
    load_share.wait()
    ga = nn(high, xs[...]) + nn(low, xs[...])
    for i in range(2):
        ga_half[i] = ga[:, i * half : (i + 1) * half]
    ga_pair = to_sibling(ga_half.at[1 - core], ga_in, 1)
    ga_pair.start()

    chip = c // 2

    def chip_copy(buf, send, recv, d):
        return pltpu.make_async_remote_copy(
            src_ref=buf.at[chip],
            dst_ref=buf.at[chip],
            send_sem=send.at[d],
            recv_sem=recv.at[chip],
            device_id={"ctx": lax.rem(c + 2 * d, n_ctx)},
            device_id_type=MESH,
        )

    def chip_arrival(buf, send, recv, d):
        other = lax.rem(chip + d, chips)
        return pltpu.make_async_remote_copy(
            src_ref=buf.at[other],
            dst_ref=buf.at[other],
            send_sem=send.at[0],
            recv_sem=recv.at[other],
            device_id={"ctx": lax.rem(c + 2 * d, n_ctx)},
            device_id_type=MESH,
        )

    gb_pair.wait_recv()
    gb_sums[chip] = gb_half[core] + gb_in[...]
    for d in range(1, chips):
        chip_copy(gb_sums, gbc_send, gbc_recv, d).start()
    ga_pair.wait_recv()
    ga_sums[chip] = (ga_half[core] + ga_in[...]).astype(BF16)
    for d in range(1, chips):
        chip_copy(ga_sums, gac_send, gac_recv, d).start()

    for d in range(1, chips):
        chip_arrival(ga_sums, gac_send, gac_recv, d).wait_recv()
    total = ga_sums[0].astype(F32)
    for i in range(1, chips):
        total = total + ga_sums[i].astype(F32)
    full[core, t] = total.astype(BF16)

    def full_copy(d):
        return pltpu.make_async_remote_copy(
            src_ref=full.at[core, t],
            dst_ref=full.at[core, t],
            send_sem=full_send.at[d],
            recv_sem=full_recv.at[t],
            device_id={"tp": lax.rem(t + d, n_tp)},
            device_id_type=MESH,
        )

    def full_arrival(s):
        return pltpu.make_async_remote_copy(
            src_ref=full.at[core, s],
            dst_ref=full.at[core, s],
            send_sem=full_send.at[0],
            recv_sem=full_recv.at[s],
            device_id={"tp": s},
            device_id_type=MESH,
        )

    for d in range(1, n_tp):
        full_copy(d).start()

    for p in range(PLACES):

        @pl.when(place == p)
        def _(p=p):
            if p in SUMMED:
                b, slot = SUMMED[p]
                term_copy(dk_out, dk_send, dk_in_recv, 5 - p, b, SUMMED).wait_recv()
                dk_out[b] = (dk_out[b].astype(F32) + dk_in[slot].astype(F32)).astype(BF16)
                term_copy(dk_out, dk_send, dk_in_recv, p, b, SUMMED).start()

    for d in range(1, chips):
        chip_arrival(gb_sums, gbc_send, gbc_recv, d).wait_recv()
    gb = gb_sums[0]
    for i in range(1, chips):
        gb = gb + gb_sums[i]
    gb_ref[core] = gb
    gb_other = to_sibling(gb_ref.at[core], gb_ref.at[core], 2)
    gb_other.start()

    gb_other.wait_recv()
    own_gb = pltpu.make_async_copy(gb_ref, gb_hbm, out_sem.at[4])
    own_gb.start()

    for d in range(1, n_tp):
        full_arrival(lax.rem(t + d, n_tp)).wait_recv()
    full_pair = to_sibling(full.at[core], full.at[core], 3)
    full_pair.start()
    own_share = pltpu.make_async_copy(full.at[core], full_hbm.at[core], out_sem.at[3])
    own_share.start()
    for p in range(PLACES):

        @pl.when(place == p)
        def _(p=p):
            total = dk_own[...]
            for src in SOURCES[p]:
                term_copy(dk_out, dk_send, dk_in_recv, src, p, SUMMED).wait_recv()
                total = total + dk_in[src - 1].astype(F32)
            gk_ref[...] = unrotate(total, pl.ds(0, rows)).astype(BF16)

    pltpu.make_async_copy(gk_ref, gk_hbm, out_sem.at[2]).start()
    full_pair.wait_recv()
    other_share = pltpu.make_async_copy(full.at[1 - core], full_hbm.at[1 - core], out_sem.at[5])
    other_share.start()

    for d in range(1, chips):
        chip_copy(gb_sums, gbc_send, gbc_recv, d).wait_send()
        chip_copy(ga_sums, gac_send, gac_recv, d).wait_send()
    for copy in (gb_pair, ga_pair, gb_other, full_pair):
        copy.wait_send()
    for d in range(1, n_tp):
        pull_copy(d).wait_send()
        hid_copy(d).wait_send()
        full_copy(d).wait_send()
    for p in range(PLACES):

        @pl.when(place == p)
        def _(p=p):
            for src, dst, send, recv in ((k_hbm, kall, k_send, k_recv), (v_hbm, vall, v_send, v_recv)):
                for i, to in enumerate(DIRECT[p]):
                    send_block(src, dst, p, to, send.at[i], recv).wait_send()
                if p in HANDED:
                    b, to = HANDED[p]
                    send_block(dst.at[block(b)], dst, b, to, send.at[2], recv).wait_send()
            for b in range(p):
                term_copy(dv_out, dv_send, dv_in_recv, p, b).wait_send()
                term_copy(dk_out, dk_send, dk_in_recv, p, b, SUMMED).wait_send()

    pltpu.make_async_copy(dqs, dq_hbm, out_sem.at[0]).wait()
    pltpu.make_async_copy(gv_ref, gv_hbm, out_sem.at[1]).wait()
    pltpu.make_async_copy(gk_ref, gk_hbm, out_sem.at[2]).wait()
    own_share.wait()
    other_share.wait()
    own_gb.wait()


def finish(dq_in, gk_in, gv_in, gb_in, full_in, dq, gk, gv, gaq, gbq, gav, gbv, dq_v, gk_v, gv_v, gb_v, full_v, ga_v, sem, out_sem):
    width = gbq.shape[1]
    rows = dq_in.shape[0]
    part = rows // finish_parts

    def piece(ref, i):
        return ref.at[pl.ds(i * part, part)]

    moves = [(piece(dq_in, i), piece(dq_v, i), piece(dq, i)) for i in range(finish_parts)]
    moves += [(gk_in, gk_v, gk), (gv_in, gv_v, gv)]
    loads = [pltpu.make_async_copy(a, b, sem.at[i]) for i, (a, b, _) in enumerate(moves)]
    stores = [pltpu.make_async_copy(b, c, out_sem.at[i]) for i, (_, b, c) in enumerate(moves)]
    n = len(moves)
    load_full = pltpu.make_async_copy(full_in, full_v, sem.at[n])
    load_gb = pltpu.make_async_copy(gb_in, gb_v, sem.at[n + 1])
    load_full.start()
    for load in loads:
        load.start()
    load_gb.start()
    for s in range(2):
        stores.append(pltpu.make_async_copy(ga_v.at[s], (gaq, gav)[s], out_sem.at[n + s]))
    load_full.wait()
    half = width // 2
    for s in range(full_in.shape[1]):
        for i in range(2):
            whole = full_v[i, s].astype(F32)
            a = s * width + i * half
            ga_v[0, :, a : a + half] = whole[:RANK]
            ga_v[1, :, a : a + half] = whole[RANK:]
    stores[n].start()
    stores[n + 1].start()
    for load, store in zip(loads, stores):
        load.wait()
        store.start()
    load_gb.wait()
    for i in range(2):
        stores.append(pltpu.make_async_copy(gb_v.at[i, :, pl.ds(0, half)], gbq.at[:, pl.ds(i * half, half)], out_sem.at[n + 2 + i]))
    stores.append(pltpu.make_async_copy(gb_v.at[0, :, pl.ds(half, FEATURES)], gbv, out_sem.at[n + 4]))
    for store in stores[n + 2 :]:
        store.start()
    for store in stores:
        store.wait()


finish_parts = 4


def shards(x, q, k, v, do, positions, down_q, up_q, down_v, up_v):
    n_ctx, n_tp = lax.axis_size("ctx"), lax.axis_size("tp")
    rows = q.shape[0]
    model = x.shape[1]
    keys = PLACES * rows
    halves = rows // CHUNK
    width = HEADS * FEATURES
    any_spec = pl.BlockSpec(memory_space=pl.ANY)
    vmem = pl.BlockSpec(memory_space=pltpu.VMEM)
    dma = pltpu.SemaphoreType.DMA
    terms = pltpu.VMEM((PLACES - 1, rows, FEATURES), BF16)
    whole = pltpu.VMEM((rows, FEATURES), F32)
    results = pl.pallas_call(
        functools.partial(kernel, n_ctx, n_tp, rows),
        out_shape=(
            jax.ShapeDtypeStruct((rows, width), BF16),
            jax.ShapeDtypeStruct((rows, FEATURES), BF16),
            jax.ShapeDtypeStruct((rows, FEATURES), BF16),
            jax.ShapeDtypeStruct((2, RANK, width // 2 + FEATURES), F32),
            jax.ShapeDtypeStruct((2, n_tp, 2 * RANK, width // 2), BF16),
        ),
        in_specs=[any_spec] * 5 + [vmem] * 5,
        out_specs=(any_spec,) * 5,
        scratch_shapes=[
            pltpu.VMEM((rows, width), BF16),
            pltpu.VMEM((rows // n_tp, model), BF16),
            pltpu.VMEM((keys, FEATURES), BF16),
            pltpu.VMEM((keys, FEATURES), BF16),
            pltpu.VMEM((FEATURES, keys), BF16),
            pltpu.VMEM((FEATURES + 2 * RANK, keys), BF16),
            pltpu.VMEM((halves, HEADS * CHUNK, FEATURES), BF16),
            pltpu.VMEM((2, halves, HEADS * CHUNK, FEATURES), BF16),
            pltpu.VMEM((halves, keys, HEADS * CHUNK), BF16),
            pltpu.VMEM((halves, keys, CHUNK), F32),
            pltpu.VMEM((2, halves * HEADS, 1, CHUNK), F32),
            pltpu.VMEM((2, halves * HEADS, 1, CHUNK), F32),
            pltpu.VMEM((rows, width), BF16),
            terms,
            terms,
            terms,
            terms,
            whole,
            whole,
            whole,
            whole,
            pltpu.VMEM((2 * RANK, model), BF16),
            pltpu.VMEM((n_tp, rows // n_tp, FEATURES), BF16),
            pltpu.VMEM((n_tp, 2 * RANK, rows), BF16),
            pltpu.VMEM((2, RANK, width // 2 + FEATURES), F32),
            pltpu.VMEM((RANK, width // 2 + FEATURES), F32),
            pltpu.VMEM((n_ctx // 2, RANK, width // 2 + FEATURES), F32),
            pltpu.VMEM((2, RANK, width // 2 + FEATURES), F32),
            pltpu.VMEM((2, 2 * RANK, width // 2), F32),
            pltpu.VMEM((2 * RANK, width // 2), F32),
            pltpu.VMEM((n_ctx // 2, 2 * RANK, width // 2), BF16),
            pltpu.VMEM((2, n_tp, 2 * RANK, width // 2), BF16),
            pltpu.VMEM((rows, FEATURES), BF16),
            pltpu.VMEM((rows, FEATURES), BF16),
            dma((2, halves * HEADS)),
            dma((2,)),
            dma((6,)),
            dma((2,)),
            dma((3,)),
            dma((PLACES,)),
            dma((3,)),
            dma((PLACES,)),
            dma((PLACES - 1,)),
            dma((PLACES - 1,)),
            dma((PLACES - 1,)),
            dma((PLACES - 1,)),
            dma((n_tp,)),
            dma((n_tp,)),
            dma((4,)),
            dma((4,)),
            dma((n_ctx // 2,)),
            dma((n_ctx // 2,)),
            dma((n_ctx // 2,)),
            dma((n_ctx // 2,)),
            dma((n_tp,)),
            dma((n_tp,)),
            dma((n_tp,)),
            dma((n_tp,)),
        ],
        compiler_params=pltpu.CompilerParams(
            collective_id=0, has_side_effects=True, vmem_limit_bytes=56 * 1024 * 1024
        ),
        cost_estimate=pl.CostEstimate(flops=12 * 10**9, bytes_accessed=16 * 10**6, transcendentals=8 * 10**6),
    )(x, q, k, v, do, positions.reshape(1, rows), down_q, up_q, down_v, up_v)
    return pl.pallas_call(
        finish,
        out_shape=(
            jax.ShapeDtypeStruct((rows, width), BF16),
            jax.ShapeDtypeStruct((rows, FEATURES), BF16),
            jax.ShapeDtypeStruct((rows, FEATURES), BF16),
            jax.ShapeDtypeStruct((RANK, model), F32),
            jax.ShapeDtypeStruct((RANK, width), F32),
            jax.ShapeDtypeStruct((RANK, model), F32),
            jax.ShapeDtypeStruct((RANK, FEATURES), F32),
        ),
        in_specs=[any_spec] * 5,
        out_specs=(any_spec,) * 7,
        scratch_shapes=[
            pltpu.VMEM((rows, width), BF16),
            pltpu.VMEM((rows, FEATURES), BF16),
            pltpu.VMEM((rows, FEATURES), BF16),
            pltpu.VMEM((2, RANK, width // 2 + FEATURES), F32),
            pltpu.VMEM((2, n_tp, 2 * RANK, width // 2), BF16),
            pltpu.VMEM((2, RANK, model), F32),
            dma((finish_parts + 4,)),
            dma((finish_parts + 7,)),
        ],
        compiler_params=pltpu.CompilerParams(vmem_limit_bytes=56 * 1024 * 1024),
    )(*results)


def solution(mesh):
    in_specs = (
        P("ctx", None),
        P("ctx", "tp"),
        P("ctx", "tp"),
        P("ctx", "tp"),
        P("ctx", "tp"),
        P("ctx"),
        P(),
        P(None, "tp"),
        P(),
        P(None, "tp"),
    )
    out_specs = (
        P("ctx", "tp"),
        P("ctx", "tp"),
        P("ctx", "tp"),
        P(),
        P(None, "tp"),
        P(),
        P(None, "tp"),
    )
    return jax.shard_map(shards, mesh=mesh, in_specs=in_specs, out_specs=out_specs, check_vma=False)
```

```python
import functools
import math

import jax
import jax.numpy as jnp
from jax import lax
from jax.experimental import pallas as pl
from jax.experimental.pallas import tpu as pltpu
from jax.sharding import PartitionSpec as P

QUERY_HEADS = 64
KEY_VALUE_HEADS = 8
FEATURES = 128
RANK = 8
SCALE_NUM = 1
SCALE_DEN = 8
ROPE_BASE = 10000.0
PLACES = 4
CHUNK = 256
HEADS = QUERY_HEADS // KEY_VALUE_HEADS
SCALE = FEATURES**-0.5
SCALE_LOG2 = SCALE * math.log2(math.e)

F32 = jnp.float32
BF16 = jnp.bfloat16
MESH = pl.DeviceIdType.MESH

SUMMED = {2: (0, 0), 3: (1, 1)}
SOURCES = {0: (1, 2), 1: (3,), 2: (3,), 3: ()}

DIRECT = {0: (1, 2), 1: (3,), 2: (3,), 3: ()}
HANDED = {2: (0, 3), 3: (1, 2)}


def nt(a, b):
    return lax.dot_general(a, b, (((1,), (1,)), ((), ())), preferred_element_type=F32)


def nn(a, b):
    return jnp.dot(a, b, preferred_element_type=F32)


def fold(a, op):
    return op(a.reshape(a.shape[0] // 8, 8, a.shape[1]), axis=0)


def kernel(
    n_ctx,
    n_tp,
    rows,
    x_hbm,
    q_hbm,
    k_hbm,
    v_hbm,
    do_hbm,
    pos_ref,
    dq_down_ref,
    up_q_ref,
    dv_down_ref,
    up_v_ref,
    dq_hbm,
    gk_hbm,
    gv_hbm,
    gb_hbm,
    full_hbm,
    xs,
    xr,
    kall,
    vall,
    ktr,
    vtr,
    qs,
    dos,
    prob,
    work,
    peaks,
    deltas,
    dqs,
    dv_out,
    dv_in,
    dk_out,
    dk_in,
    dv_own,
    dk_own,
    ctab,
    stab,
    down,
    hid,
    pulls,
    gb_half,
    gb_in,
    gb_sums,
    gb_ref,
    ga_half,
    ga_in,
    ga_sums,
    full,
    gk_ref,
    gv_ref,
    load_sem,
    xsem,
    out_sem,
    own_sem,
    k_send,
    k_recv,
    v_send,
    v_recv,
    dv_send,
    dv_recv,
    dk_send,
    dk_recv,
    pull_send,
    pull_recv,
    sib_send,
    sib_recv,
    gbc_send,
    gbc_recv,
    gac_send,
    gac_recv,
    full_send,
    full_recv,
    hid_send,
    hid_recv,
):
    c = lax.axis_index("ctx")
    t = lax.axis_index("tp")
    halves = rows // CHUNK
    width = HEADS * FEATURES
    shifted = jnp.where(t >= n_tp // 2, PLACES // 2, 0)
    place = lax.rem(c + shifted, PLACES)

    def member(j):
        return lax.rem(c - place + j + n_ctx, n_ctx)

    barrier = pltpu.get_barrier_semaphore()
    core = lax.rem(c, 2)
    sibling = c + 1 - 2 * core
    chips = n_ctx // 2
    for peer in [sibling, member(PLACES - 1 - place)] + [lax.rem(c + 2 * d, n_ctx) for d in range(1, chips)]:
        pl.semaphore_signal(barrier, inc=1, device_id={"ctx": peer}, device_id_type=MESH)
    for d in range(1, n_tp):
        pl.semaphore_signal(barrier, inc=1, device_id={"tp": lax.rem(t + d, n_tp)}, device_id_type=MESH)

    own = pl.ds(pl.multiple_of(place * rows, rows), rows)
    own_k = pltpu.make_async_copy(k_hbm, kall.at[own], own_sem.at[0])
    own_v = pltpu.make_async_copy(v_hbm, vall.at[own], own_sem.at[1])
    own_k.start()
    loads = []
    for j in range(halves):
        for h in range(HEADS):
            for n, (src, dst) in enumerate(((q_hbm, qs), (do_hbm, dos.at[1]))):
                loads.append(
                    pltpu.make_async_copy(
                        src.at[pl.ds(j * CHUNK, CHUNK), pl.ds(h * FEATURES, FEATURES)],
                        dst.at[j, pl.ds(h * CHUNK, CHUNK)],
                        load_sem.at[n, j * HEADS + h],
                    )
                )
    part = rows // n_tp
    load_rows = pltpu.make_async_copy(x_hbm.at[pl.ds(pl.multiple_of(t * part, part), part)], xr, xsem.at[0])
    load_share = pltpu.make_async_copy(x_hbm.at[:, pl.ds(pl.multiple_of(t * width, width), width)], xs, xsem.at[1])
    load_rows.start()
    for copy in loads:
        copy.start()
    own_v.start()
    load_share.start()

    pl.semaphore_wait(barrier, chips + n_tp)

    def block(b):
        return pl.ds(b * rows, rows)

    def send_block(src, dst, b, to, send, recv):
        return pltpu.make_async_remote_copy(
            src_ref=src,
            dst_ref=dst.at[block(b)],
            send_sem=send,
            recv_sem=recv.at[b],
            device_id={"ctx": member(to)},
            device_id_type=MESH,
        )

    for p in range(PLACES):

        @pl.when(place == p)
        def _(p=p):
            for i, to in enumerate(DIRECT[p]):
                send_block(k_hbm, kall, p, to, k_send.at[i], k_recv).start()

    index = lax.broadcasted_iota(jnp.int32, (FEATURES // 2, rows), 0).astype(F32)
    inverse = jnp.exp(index * (-2.0 / FEATURES) * jnp.log(F32(ROPE_BASE)))
    angle = ((pos_ref[...] * SCALE_NUM).astype(F32) / SCALE_DEN) * inverse
    cosine, sine = jnp.cos(angle), jnp.sin(angle)
    ctab[...] = jnp.concatenate([cosine, cosine], axis=0).T
    stab[...] = jnp.concatenate([sine, -sine], axis=0).T

    ones = lax.broadcasted_iota(jnp.int32, (2 * RANK, PLACES * rows), 0) == 0
    vtr[FEATURES:, :] = jnp.where(ones, 1.0, 0.0).astype(BF16)
    down[...] = jnp.concatenate([dq_down_ref[...].astype(F32), dv_down_ref[...].astype(F32)], axis=0).astype(BF16)
    load_rows.wait()
    h = nt(xr[...], down[...])
    hid[t] = jnp.concatenate([h, jnp.zeros((part, FEATURES - 2 * RANK), F32)], axis=1).astype(BF16)

    def hid_copy(d):
        return pltpu.make_async_remote_copy(
            src_ref=hid.at[t],
            dst_ref=hid.at[t],
            send_sem=hid_send.at[d],
            recv_sem=hid_recv.at[t],
            device_id={"tp": lax.rem(t + d, n_tp)},
            device_id_type=MESH,
        )

    def hid_arrival(s):
        return pltpu.make_async_remote_copy(
            src_ref=hid.at[s],
            dst_ref=hid.at[s],
            send_sem=hid_send.at[0],
            recv_sem=hid_recv.at[s],
            device_id={"tp": s},
            device_id_type=MESH,
        )

    for d in range(1, n_tp):
        hid_copy(d).start()
    for p in range(PLACES):

        @pl.when(place == p)
        def _(p=p):
            for i, to in enumerate(DIRECT[p]):
                send_block(v_hbm, vall, p, to, v_send.at[i], v_recv).start()

    for copy in loads:
        copy.wait()
    own_k.wait()
    own_v.wait()

    causal = lax.broadcasted_iota(jnp.int32, (CHUNK, CHUNK), 0) <= lax.broadcasted_iota(jnp.int32, (CHUNK, CHUNK), 1)

    def unrotate(a, tokens):
        return a * ctab[tokens, :] + pltpu.roll(a, FEATURES // 2, 1) * stab[tokens, :]

    def spans_of(p):
        spans = [(0, 0, 2 * rows), (1, 2 * rows, None)] if p >= 2 else [(1, 0, None)]

        def span(g, j):
            _, a, b = next(s for s in spans if s[0] == g)
            return a, (halves * p + j + 1) * CHUNK if b is None else b

        return spans, span

    def attention(p):
        def tiles(j):
            return halves * p + j + 1

        def take(i):
            return pl.ds(i * CHUNK, CHUNK)

        def arrive(dst, send, recv, kind, done=None):
            src = k_hbm if kind == 0 else v_hbm
            if p in HANDED:
                b, to = HANDED[p]
                send_block(src, dst, b, to, send.at[2], recv).wait_recv()
                send_block(dst.at[block(b)], dst, b, to, send.at[2], recv).start()
            for b in range(p):
                if b != done and (p not in HANDED or b != HANDED[p][0]):
                    send_block(src, dst, b, b, send.at[0], recv).wait_recv()

        spans, span = spans_of(p)

        def softmax(g):
            @pl.loop(0, HEADS // 2)
            def _(h0):
                for h in [h0 * 2 + i for i in range(2)]:
                    cols = pl.ds(pl.multiple_of(h * CHUNK, CHUNK), CHUNK)
                    for j in range(halves):
                        query = qs[j, cols, :]
                        first, end = span(g, j)
                        last = end - CHUNK if g else end
                        starts = list(range(first, last, 2 * CHUNK)) + [last] * (g == 1)
                        peak = None
                        for a, b in zip(starts, starts[1:] + [end]):
                            s = nt(kall[a:b, :], query)
                            if g and a == last:
                                s = jnp.where(causal, s, -1e30)
                            work[j, a:b, :] = s
                            top = fold(s, jnp.max)
                            peak = top if peak is None else jnp.maximum(peak, top)
                        peak = jnp.max(peak, axis=0, keepdims=True) * SCALE_LOG2
                        peaks[g, j * HEADS + h] = peak
                        for a in range(first, end, CHUNK):
                            b = a + CHUNK
                            prob[j, a:b, cols] = jnp.exp2(work[j, a:b, :] * SCALE_LOG2 - peak).astype(BF16)

        near = {1: 0, 3: 2}
        if p in near:
            send_block(k_hbm, kall, near[p], near[p], k_send.at[0], k_recv).wait_recv()
        softmax(1)
        arrive(kall, k_send, k_recv, 0, near.get(p))
        for i in range(halves * (p + 1)):
            ktr[:, take(i)] = kall[take(i), :].T
        if p >= 2:
            softmax(0)

        arrive(vall, v_send, v_recv, 1)
        for i in range(halves * (p + 1)):
            vtr[:FEATURES, take(i)] = vall[take(i), :].T

        @pl.loop(0, HEADS // 2)
        def _(h0):
            for h in [h0 * 2 + i for i in range(2)]:
                cols = pl.ds(pl.multiple_of(h * CHUNK, CHUNK), CHUNK)
                for j in range(halves):
                    u = j * HEADS + h
                    outs = {}
                    for g, _, _ in spans:
                        a, b = span(g, j)
                        outs[g] = nn(vtr[:, a:b], prob[j, a:b, cols])
                    if p >= 2:
                        peak = jnp.maximum(peaks[0, u], peaks[1, u])
                        factor = {g: jnp.exp2(peaks[g, u] - peak) for g in outs}
                        out = outs[0] * factor[0] + outs[1] * factor[1]
                        inv = 1.0 / out[FEATURES : FEATURES + 1]
                        factor = {g: factor[g] * inv for g in outs}
                    else:
                        out = outs[1]
                        inv = 1.0 / out[FEATURES : FEATURES + 1]
                        factor = {1: inv}
                    up = dos[1, j, cols, :].T.astype(F32)
                    delta = jnp.sum(up * out[:FEATURES], axis=0, keepdims=True) * inv
                    for g in outs:
                        deltas[g, u] = delta * factor[g]
                        dos[g, j, cols, :] = (up * factor[g]).astype(BF16).T

    def query_terms(p):
        def tiles(j):
            return halves * p + j + 1

        def take(i):
            return pl.ds(i * CHUNK, CHUNK)

        spans, span = spans_of(p)

        @pl.loop(0, HEADS // 2)
        def _(h0):
            for h in [h0 * 2 + i for i in range(2)]:
                cols = pl.ds(pl.multiple_of(h * CHUNK, CHUNK), CHUNK)
                for j in range(halves):
                    length = tiles(j) * CHUNK
                    for g, _, _ in spans:
                        up = dos[g, j, cols, :]
                        delta = deltas[g, j * HEADS + h]
                        first, end = span(g, j)
                        for a in range(first, end, 4 * CHUNK):
                            b = min(a + 4 * CHUNK, end)
                            m = nt(vall[a:b, :], up)
                            prob[j, a:b, cols] = (prob[j, a:b, cols].astype(F32) * (m - delta)).astype(BF16)
                    grad = nn(ktr[:, :length], prob[j, :length, cols])
                    out = unrotate(grad.T * SCALE, take(j))
                    dqs[take(j), pl.ds(pl.multiple_of(h * FEATURES, FEATURES), FEATURES)] = out.astype(BF16)

    def key_terms(right, scale, outs, send, into, kept, summed):
        def finish(a):
            return a if scale is None else a * scale

        def product(first, length, j, g):
            return nn(prob[j, pl.ds(pl.multiple_of(first, CHUNK), length), :], right(j, g))

        def other(b, carry):
            g = jnp.where((place >= 2) & (b < 2), 0, 1)
            a = product(b * rows, rows, 0, g)
            for j in range(1, halves):
                a = a + product(b * rows, rows, j, g)
            outs[b] = finish(a).astype(BF16)
            dst, recv = into
            held = place < 0
            to, slot = b, place - 1
            if summed:
                cross = (place >= 2) & (b < 2)
                held = cross & (b == place - 2)
                to, slot = jnp.where(cross, 5 - place, b), jnp.where(cross, b, place - 1)

            @pl.when(jnp.logical_not(held))
            def _():
                pltpu.make_async_remote_copy(
                    src_ref=outs.at[b],
                    dst_ref=dst.at[slot],
                    send_sem=send.at[b],
                    recv_sem=recv.at[slot],
                    device_id={"ctx": member(to)},
                    device_id_type=MESH,
                ).start()

            return carry

        lax.fori_loop(0, place, other, 0)
        for i in range(halves):
            a = None
            for j in range(i, halves):
                m = product(place * rows + i * CHUNK, CHUNK, j, 1)
                a = m if a is None else a + m
            kept[pl.ds(i * CHUNK, CHUNK), :] = finish(a)

    dv_in_recv = (dv_in, dv_recv)
    dk_in_recv = (dk_in, dk_recv)

    def term_copy(outs, send, into, src, b, summed=()):
        dst, recv = into
        to, slot = b, src - 1
        if src in summed and b == summed[5 - src][0]:
            to, slot = 5 - src, summed[5 - src][1]
        return pltpu.make_async_remote_copy(
            src_ref=outs.at[b],
            dst_ref=dst.at[slot],
            send_sem=send.at[b],
            recv_sem=recv.at[slot],
            device_id={"ctx": member(to)},
            device_id_type=MESH,
        )

    def pull_copy(d):
        return pltpu.make_async_remote_copy(
            src_ref=pulls.at[t],
            dst_ref=pulls.at[t],
            send_sem=pull_send.at[d],
            recv_sem=pull_recv.at[t],
            device_id={"tp": lax.rem(t + d, n_tp)},
            device_id_type=MESH,
        )

    def pull_arrival(s):
        return pltpu.make_async_remote_copy(
            src_ref=pulls.at[s],
            dst_ref=pulls.at[s],
            send_sem=pull_send.at[0],
            recv_sem=pull_recv.at[s],
            device_id={"tp": s},
            device_id_type=MESH,
        )

    for p in range(PLACES):
        pl.when(place == p)(functools.partial(attention, p))
    key_terms(lambda j, g: dos[g, j], None, dv_out, dv_send, dv_in_recv, dv_own, False)
    for p in range(PLACES):
        pl.when(place == p)(functools.partial(query_terms, p))
    pltpu.make_async_copy(dqs, dq_hbm, out_sem.at[0]).start()

    for p in range(PLACES):

        @pl.when(place == p)
        def _(p=p):
            total = dv_own[...]
            for src in range(p + 1, PLACES):
                term_copy(dv_out, dv_send, dv_in_recv, src, p).wait_recv()
                total = total + dv_in[src - 1].astype(F32)
            gv_ref[...] = total.astype(BF16)

    pltpu.make_async_copy(gv_ref, gv_hbm, out_sem.at[1]).start()

    pull = jnp.concatenate([nt(up_q_ref[...], dqs[...]), nt(up_v_ref[...], gv_ref[...])], axis=0)
    pulls[t] = pull.astype(BF16)
    for d in range(1, n_tp):
        pull_copy(d).start()

    for d in range(1, n_tp):
        hid_arrival(lax.rem(t + d, n_tp)).wait_recv()
    hidden = hid[...].astype(F32).reshape(rows, FEATURES).T[: 2 * RANK].astype(BF16)
    gb = nn(hidden, dqs[...])[:RANK]
    gbv = nn(hidden, gv_ref[...])[RANK:]
    half = width // 2
    for i in range(2):
        gb_half[i, :, :half] = gb[:, i * half : (i + 1) * half]
        gb_half[i, :, half:] = gbv

    def to_sibling(src, dst, n):
        return pltpu.make_async_remote_copy(
            src_ref=src,
            dst_ref=dst,
            send_sem=sib_send.at[n],
            recv_sem=sib_recv.at[n],
            device_id={"ctx": sibling},
            device_id_type=MESH,
        )

    gb_pair = to_sibling(gb_half.at[1 - core], gb_in, 0)
    gb_pair.start()

    key_terms(lambda j, g: qs[j], SCALE, dk_out, dk_send, dk_in_recv, dk_own, True)

    for d in range(1, n_tp):
        pull_arrival(lax.rem(t + d, n_tp)).wait_recv()
    pull = pulls[0].astype(F32)
    for s in range(1, n_tp):
        pull = pull + pulls[s].astype(F32)
    high = pull.astype(BF16)
    low = (pull - high.astype(F32)).astype(BF16)
    load_share.wait()
    ga = nn(high, xs[...]) + nn(low, xs[...])
    for i in range(2):
        ga_half[i] = ga[:, i * half : (i + 1) * half]
    ga_pair = to_sibling(ga_half.at[1 - core], ga_in, 1)
    ga_pair.start()

    chip = c // 2

    def chip_copy(buf, send, recv, d):
        return pltpu.make_async_remote_copy(
            src_ref=buf.at[chip],
            dst_ref=buf.at[chip],
            send_sem=send.at[d],
            recv_sem=recv.at[chip],
            device_id={"ctx": lax.rem(c + 2 * d, n_ctx)},
            device_id_type=MESH,
        )

    def chip_arrival(buf, send, recv, d):
        other = lax.rem(chip + d, chips)
        return pltpu.make_async_remote_copy(
            src_ref=buf.at[other],
            dst_ref=buf.at[other],
            send_sem=send.at[0],
            recv_sem=recv.at[other],
            device_id={"ctx": lax.rem(c + 2 * d, n_ctx)},
            device_id_type=MESH,
        )

    gb_pair.wait_recv()
    gb_sums[chip] = gb_half[core] + gb_in[...]
    for d in range(1, chips):
        chip_copy(gb_sums, gbc_send, gbc_recv, d).start()
    ga_pair.wait_recv()
    ga_sums[chip] = (ga_half[core] + ga_in[...]).astype(BF16)
    for d in range(1, chips):
        chip_copy(ga_sums, gac_send, gac_recv, d).start()

    for d in range(1, chips):
        chip_arrival(ga_sums, gac_send, gac_recv, d).wait_recv()
    total = ga_sums[0].astype(F32)
    for i in range(1, chips):
        total = total + ga_sums[i].astype(F32)
    full[core, t] = total.astype(BF16)

    def full_copy(d):
        return pltpu.make_async_remote_copy(
            src_ref=full.at[core, t],
            dst_ref=full.at[core, t],
            send_sem=full_send.at[d],
            recv_sem=full_recv.at[t],
            device_id={"tp": lax.rem(t + d, n_tp)},
            device_id_type=MESH,
        )

    def full_arrival(s):
        return pltpu.make_async_remote_copy(
            src_ref=full.at[core, s],
            dst_ref=full.at[core, s],
            send_sem=full_send.at[0],
            recv_sem=full_recv.at[s],
            device_id={"tp": s},
            device_id_type=MESH,
        )

    for d in range(1, n_tp):
        full_copy(d).start()

    for p in range(PLACES):

        @pl.when(place == p)
        def _(p=p):
            if p in SUMMED:
                b, slot = SUMMED[p]
                term_copy(dk_out, dk_send, dk_in_recv, 5 - p, b, SUMMED).wait_recv()
                dk_out[b] = (dk_out[b].astype(F32) + dk_in[slot].astype(F32)).astype(BF16)
                term_copy(dk_out, dk_send, dk_in_recv, p, b, SUMMED).start()

    for d in range(1, chips):
        chip_arrival(gb_sums, gbc_send, gbc_recv, d).wait_recv()
    gb = gb_sums[0]
    for i in range(1, chips):
        gb = gb + gb_sums[i]
    gb_ref[core] = gb
    gb_other = to_sibling(gb_ref.at[core], gb_ref.at[core], 2)
    gb_other.start()

    gb_other.wait_recv()
    own_gb = pltpu.make_async_copy(gb_ref, gb_hbm, out_sem.at[4])
    own_gb.start()

    for d in range(1, n_tp):
        full_arrival(lax.rem(t + d, n_tp)).wait_recv()
    full_pair = to_sibling(full.at[core], full.at[core], 3)
    full_pair.start()
    own_share = pltpu.make_async_copy(full.at[core], full_hbm.at[core], out_sem.at[3])
    own_share.start()
    for p in range(PLACES):

        @pl.when(place == p)
        def _(p=p):
            total = dk_own[...]
            for src in SOURCES[p]:
                term_copy(dk_out, dk_send, dk_in_recv, src, p, SUMMED).wait_recv()
                total = total + dk_in[src - 1].astype(F32)
            gk_ref[...] = unrotate(total, pl.ds(0, rows)).astype(BF16)

    pltpu.make_async_copy(gk_ref, gk_hbm, out_sem.at[2]).start()
    full_pair.wait_recv()
    other_share = pltpu.make_async_copy(full.at[1 - core], full_hbm.at[1 - core], out_sem.at[5])
    other_share.start()

    for d in range(1, chips):
        chip_copy(gb_sums, gbc_send, gbc_recv, d).wait_send()
        chip_copy(ga_sums, gac_send, gac_recv, d).wait_send()
    for copy in (gb_pair, ga_pair, gb_other, full_pair):
        copy.wait_send()
    for d in range(1, n_tp):
        pull_copy(d).wait_send()
        hid_copy(d).wait_send()
        full_copy(d).wait_send()
    for p in range(PLACES):

        @pl.when(place == p)
        def _(p=p):
            for src, dst, send, recv in ((k_hbm, kall, k_send, k_recv), (v_hbm, vall, v_send, v_recv)):
                for i, to in enumerate(DIRECT[p]):
                    send_block(src, dst, p, to, send.at[i], recv).wait_send()
                if p in HANDED:
                    b, to = HANDED[p]
                    send_block(dst.at[block(b)], dst, b, to, send.at[2], recv).wait_send()
            for b in range(p):
                term_copy(dv_out, dv_send, dv_in_recv, p, b).wait_send()
                term_copy(dk_out, dk_send, dk_in_recv, p, b, SUMMED).wait_send()

    pltpu.make_async_copy(dqs, dq_hbm, out_sem.at[0]).wait()
    pltpu.make_async_copy(gv_ref, gv_hbm, out_sem.at[1]).wait()
    pltpu.make_async_copy(gk_ref, gk_hbm, out_sem.at[2]).wait()
    own_share.wait()
    other_share.wait()
    own_gb.wait()


def finish(dq_in, gk_in, gv_in, gb_in, full_in, dq, gk, gv, gaq, gbq, gav, gbv, dq_v, gk_v, gv_v, gb_v, full_v, ga_v, sem, out_sem):
    width = gbq.shape[1]
    rows = dq_in.shape[0]
    part = rows // finish_parts

    def piece(ref, i):
        return ref.at[pl.ds(i * part, part)]

    moves = [(piece(dq_in, i), piece(dq_v, i), piece(dq, i)) for i in range(finish_parts)]
    moves += [(gk_in, gk_v, gk), (gv_in, gv_v, gv)]
    loads = [pltpu.make_async_copy(a, b, sem.at[i]) for i, (a, b, _) in enumerate(moves)]
    stores = [pltpu.make_async_copy(b, c, out_sem.at[i]) for i, (_, b, c) in enumerate(moves)]
    n = len(moves)
    load_full = pltpu.make_async_copy(full_in, full_v, sem.at[n])
    load_gb = pltpu.make_async_copy(gb_in, gb_v, sem.at[n + 1])
    load_full.start()
    for load in loads:
        load.start()
    load_gb.start()
    for s in range(2):
        stores.append(pltpu.make_async_copy(ga_v.at[s], (gaq, gav)[s], out_sem.at[n + s]))
    load_full.wait()
    half = width // 2
    for s in range(full_in.shape[1]):
        for i in range(2):
            whole = full_v[i, s].astype(F32)
            a = s * width + i * half
            ga_v[0, :, a : a + half] = whole[:RANK]
            ga_v[1, :, a : a + half] = whole[RANK:]
    stores[n].start()
    stores[n + 1].start()
    for load, store in zip(loads, stores):
        load.wait()
        store.start()
    load_gb.wait()
    for i in range(2):
        stores.append(pltpu.make_async_copy(gb_v.at[i, :, pl.ds(0, half)], gbq.at[:, pl.ds(i * half, half)], out_sem.at[n + 2 + i]))
    stores.append(pltpu.make_async_copy(gb_v.at[0, :, pl.ds(half, FEATURES)], gbv, out_sem.at[n + 4]))
    for store in stores[n + 2 :]:
        store.start()
    for store in stores:
        store.wait()


finish_parts = 4


def shards(x, q, k, v, do, positions, down_q, up_q, down_v, up_v):
    n_ctx, n_tp = lax.axis_size("ctx"), lax.axis_size("tp")
    rows = q.shape[0]
    model = x.shape[1]
    keys = PLACES * rows
    halves = rows // CHUNK
    width = HEADS * FEATURES
    any_spec = pl.BlockSpec(memory_space=pl.ANY)
    vmem = pl.BlockSpec(memory_space=pltpu.VMEM)
    dma = pltpu.SemaphoreType.DMA
    terms = pltpu.VMEM((PLACES - 1, rows, FEATURES), BF16)
    whole = pltpu.VMEM((rows, FEATURES), F32)
    results = pl.pallas_call(
        functools.partial(kernel, n_ctx, n_tp, rows),
        out_shape=(
            jax.ShapeDtypeStruct((rows, width), BF16),
            jax.ShapeDtypeStruct((rows, FEATURES), BF16),
            jax.ShapeDtypeStruct((rows, FEATURES), BF16),
            jax.ShapeDtypeStruct((2, RANK, width // 2 + FEATURES), F32),
            jax.ShapeDtypeStruct((2, n_tp, 2 * RANK, width // 2), BF16),
        ),
        in_specs=[any_spec] * 5 + [vmem] * 5,
        out_specs=(any_spec,) * 5,
        scratch_shapes=[
            pltpu.VMEM((rows, width), BF16),
            pltpu.VMEM((rows // n_tp, model), BF16),
            pltpu.VMEM((keys, FEATURES), BF16),
            pltpu.VMEM((keys, FEATURES), BF16),
            pltpu.VMEM((FEATURES, keys), BF16),
            pltpu.VMEM((FEATURES + 2 * RANK, keys), BF16),
            pltpu.VMEM((halves, HEADS * CHUNK, FEATURES), BF16),
            pltpu.VMEM((2, halves, HEADS * CHUNK, FEATURES), BF16),
            pltpu.VMEM((halves, keys, HEADS * CHUNK), BF16),
            pltpu.VMEM((halves, keys, CHUNK), F32),
            pltpu.VMEM((2, halves * HEADS, 1, CHUNK), F32),
            pltpu.VMEM((2, halves * HEADS, 1, CHUNK), F32),
            pltpu.VMEM((rows, width), BF16),
            terms,
            terms,
            terms,
            terms,
            whole,
            whole,
            whole,
            whole,
            pltpu.VMEM((2 * RANK, model), BF16),
            pltpu.VMEM((n_tp, rows // n_tp, FEATURES), BF16),
            pltpu.VMEM((n_tp, 2 * RANK, rows), BF16),
            pltpu.VMEM((2, RANK, width // 2 + FEATURES), F32),
            pltpu.VMEM((RANK, width // 2 + FEATURES), F32),
            pltpu.VMEM((n_ctx // 2, RANK, width // 2 + FEATURES), F32),
            pltpu.VMEM((2, RANK, width // 2 + FEATURES), F32),
            pltpu.VMEM((2, 2 * RANK, width // 2), F32),
            pltpu.VMEM((2 * RANK, width // 2), F32),
            pltpu.VMEM((n_ctx // 2, 2 * RANK, width // 2), BF16),
            pltpu.VMEM((2, n_tp, 2 * RANK, width // 2), BF16),
            pltpu.VMEM((rows, FEATURES), BF16),
            pltpu.VMEM((rows, FEATURES), BF16),
            dma((2, halves * HEADS)),
            dma((2,)),
            dma((6,)),
            dma((2,)),
            dma((3,)),
            dma((PLACES,)),
            dma((3,)),
            dma((PLACES,)),
            dma((PLACES - 1,)),
            dma((PLACES - 1,)),
            dma((PLACES - 1,)),
            dma((PLACES - 1,)),
            dma((n_tp,)),
            dma((n_tp,)),
            dma((4,)),
            dma((4,)),
            dma((n_ctx // 2,)),
            dma((n_ctx // 2,)),
            dma((n_ctx // 2,)),
            dma((n_ctx // 2,)),
            dma((n_tp,)),
            dma((n_tp,)),
            dma((n_tp,)),
            dma((n_tp,)),
        ],
        compiler_params=pltpu.CompilerParams(
            collective_id=0, has_side_effects=True, vmem_limit_bytes=56 * 1024 * 1024
        ),
        cost_estimate=pl.CostEstimate(flops=12 * 10**9, bytes_accessed=16 * 10**6, transcendentals=8 * 10**6),
    )(x, q, k, v, do, positions.reshape(1, rows), down_q, up_q, down_v, up_v)
    return pl.pallas_call(
        finish,
        out_shape=(
            jax.ShapeDtypeStruct((rows, width), BF16),
            jax.ShapeDtypeStruct((rows, FEATURES), BF16),
            jax.ShapeDtypeStruct((rows, FEATURES), BF16),
            jax.ShapeDtypeStruct((RANK, model), F32),
            jax.ShapeDtypeStruct((RANK, width), F32),
            jax.ShapeDtypeStruct((RANK, model), F32),
            jax.ShapeDtypeStruct((RANK, FEATURES), F32),
        ),
        in_specs=[any_spec] * 5,
        out_specs=(any_spec,) * 7,
        scratch_shapes=[
            pltpu.VMEM((rows, width), BF16),
            pltpu.VMEM((rows, FEATURES), BF16),
            pltpu.VMEM((rows, FEATURES), BF16),
            pltpu.VMEM((2, RANK, width // 2 + FEATURES), F32),
            pltpu.VMEM((2, n_tp, 2 * RANK, width // 2), BF16),
            pltpu.VMEM((2, RANK, model), F32),
            dma((finish_parts + 4,)),
            dma((finish_parts + 7,)),
        ],
        compiler_params=pltpu.CompilerParams(vmem_limit_bytes=56 * 1024 * 1024),
    )(*results)


def solution(mesh):
    in_specs = (
        P("ctx", None),
        P("ctx", "tp"),
        P("ctx", "tp"),
        P("ctx", "tp"),
        P("ctx", "tp"),
        P("ctx"),
        P(),
        P(None, "tp"),
        P(),
        P(None, "tp"),
    )
    out_specs = (
        P("ctx", "tp"),
        P("ctx", "tp"),
        P("ctx", "tp"),
        P(),
        P(None, "tp"),
        P(),
        P(None, "tp"),
    )
    return jax.shard_map(shards, mesh=mesh, in_specs=in_specs, out_specs=out_specs, check_vma=False)
```
